32 devices in a mesh: groups: 2 (over x), view: 16 (over z, y, core).
Axes of the slice: x: 2, y: 2, z: 4, core: 2. Of those that a mesh axis runs over, the one named last changes fastest.
Arguments:
- estimate: float32 [6144, 128], P(('groups', 'view')), parts along dimension 0, may hold values from 0.5 to 2, as said below
- measured: bfloat16 [512, 192, 128], P(('groups', 'view')), parts along dimension 0, may hold values from 0.25 to 4, as said below
- kernel_z: bfloat16 [16, 3, 128, 128], replicated, may hold values from 0 to 2, as said below
- kernel_x: bfloat16 [16, 3, 12, 12], replicated, may hold values from 0 to 2, as said below
- kernel_y: bfloat16 [16, 3, 16, 16], replicated, may hold values from 0 to 2, as said below
- background: bfloat16 [16], replicated, may hold values from 0.049804688 to 0.5
- relax: bfloat16 [16], replicated, may hold values from 0.029907227 to 0.23925781
- owner: int32 [512, 1], P(('groups', 'view')), parts along dimension 0, may hold values from 0 to 15; in each aligned block of 16 rows (0 to 15, 16 to 31, ...) at most 2 rows name the same one
- source_offset: int32 [512], P(('groups', 'view')), parts along dimension 0, may hold values from 0 to 184
- tile_offset: int32 [512], P(('groups', 'view')), parts along dimension 0, may hold values from 0 to 56
- feather: int32 [512, 8], P(('groups', 'view')), parts along dimension 0, may hold values from 1 to 8
Outputs:
- refined: float32 [6144, 128], P(('groups', 'view')), parts along dimension 0
- smoothed: float32 [2048, 128], P(('groups', 'view')), parts along dimension 0
The draws below stay inside these ranges and needn't reach their ends.
There are 2 independent parts, one for each index of `groups`. The reference program is written for one: setup_inputs(seed, part) draws one part's arguments, and reference() takes and returns one part's arrays. A program takes and returns all parts, laid end to end along the dimension named above; an argument that names none is the same for every part. Nothing has to cross between parts.
Inputs may be any that keep to these rules, and one draw needn't show every extreme that they name: `owner`: within the 16 rows of one block no tile is named more than 2 times, and in every draw some tile is named exactly 2 times by some block. `kernel_z`: entries are nonnegative and every diagonal entry is positive. `kernel_x`: entries are nonnegative and every diagonal entry is positive. `kernel_y`: entries are nonnegative and every diagonal entry is positive. `estimate`: entries are positive. `measured`: entries are positive.
All inputs are finite; a program needn't handle non-finite values.
Results may differ from the reference program's by a relative error of at most 0.0006.
Values may be sent and summed in bfloat16 or wider, within the bound.
No kernel may reach another device: no remote copies, remote signals or barrier semaphores. Data moves between devices by JAX's collectives and lax.ppermute only.
A program may use at most 64 MiB of HBM per device.

```python
import math
import jax
import jax.numpy as jnp
import numpy as np
from jax import lax

BX = 12
BY = 16
BZ = 128
VIEWS = 16
RANK = 3
SROWS = 8
TROWS = 64
CAP = 2
BLOCKS = 16
ROWS = 192
LIST = 16


def draw_kernel(key, extent):
    key_spread, key_factor = jax.random.split(key)
    spread = jnp.exp(jax.random.uniform(key_spread, (VIEWS, RANK, 1, 1), jnp.float32, jnp.log(0.7), jnp.log(3.0)))
    positions = jnp.arange(extent, dtype=jnp.float32)
    spacing = positions[:, None] - positions[None, :]
    profile = jnp.exp(-spacing * spacing / (2.0 * spread * spread))
    profile = profile / jnp.sum(profile, axis=-1, keepdims=True)
    factor = jax.random.uniform(key_factor, (VIEWS, RANK, extent, extent), jnp.float32, 0.5, 1.5)
    return (0.7 * profile * factor).astype(jnp.bfloat16)


def draw_kernel_z(key, part):
    return draw_kernel(jax.random.fold_in(key, 31), BZ)


def draw_kernel_x(key, part):
    return draw_kernel(jax.random.fold_in(key, 37), BX)


def draw_kernel_y(key, part):
    return draw_kernel(jax.random.fold_in(key, 41), BY)


def draw_estimate(key, part):
    key_rough = jax.random.fold_in(jax.random.fold_in(key, 43), 0)
    rough = jax.random.uniform(key_rough, (BLOCKS * ROWS, BZ), jnp.float32, jnp.log(0.5), jnp.log(2.0))
    values = jnp.exp(rough)
    return jnp.clip(values, 0.5, 2.0).astype(jnp.float32)


def draw_measured(key, part):
    key_rough = jax.random.fold_in(jax.random.fold_in(key, 47), 0)
    rough = jax.random.uniform(key_rough, (BLOCKS * VIEWS, ROWS, BZ), jnp.float32, jnp.log(0.5), jnp.log(2.0))
    values = jnp.exp(rough)
    return jnp.clip(values, 0.25, 4.0).astype(jnp.bfloat16)


def set_ends(result, own_key, least, largest):
    shape = result.shape
    spot = [jax.random.randint(jax.random.fold_in(own_key, axis), (), 0, shape[axis]) for axis in range(len(shape))]
    result = result.at[tuple(spot)].set(least)
    longest = shape.index(max(shape))
    spot[longest] = (spot[longest] + 1) % shape[longest]
    return result.at[tuple(spot)].set(largest)


def assign_block(own_key, own, number, rows, amount, top, reach, slope):
    ranking = jax.random.permutation(own_key, amount)
    crowded, usual = load_shares(amount, rows * top, reach, slope, True), load_shares(amount, rows * top, reach, slope, False)
    places = jnp.arange(amount)

    def named(sizes, offset_by):
        used = int((sizes > 0).sum())
        fixed = max(1, used // 4)
        moved = fixed + (places - fixed + offset_by * (used - fixed)) % max(1, amount - fixed)
        return jnp.zeros((amount,), jnp.int32).at[ranking[jnp.where(places < fixed, places, moved)]].set(jnp.asarray(sizes, jnp.int32))

    sizes = jnp.where(number % 4 == 0, named(crowded, number // 4), named(usual, number - number // 4 - 1))
    mixed = jax.random.permutation(jax.random.fold_in(own, 3), amount)
    donor, receiver = mixed[0:amount // 2 * 2:2], mixed[1:amount // 2 * 2:2]
    room = jnp.minimum(sizes[donor] - 1, reach - sizes[receiver]) // 2
    room = jnp.where((donor == ranking[0]) | (receiver == ranking[0]) | (sizes[receiver] == 0), 0, jnp.maximum(room, 0))
    moved = jax.random.randint(jax.random.fold_in(own, 4), (amount // 2,), 0, 1 << 20) % (room + 1)
    sizes = sizes.at[donor].add(-moved).at[receiver].add(moved)
    items = jnp.searchsorted(jnp.cumsum(sizes), jnp.arange(rows * top), side="right").astype(jnp.int32)
    listing = items.reshape(top, rows).T
    listing = listing[jax.random.permutation(jax.random.fold_in(own, 1), rows)]
    offset_by = jax.random.randint(jax.random.fold_in(own, 2), (rows, 1), 0, top)
    return jnp.take_along_axis(listing, (jnp.arange(top)[None, :] + offset_by) % top, axis=1)


def load_shares(amount, total, bound, slope, full):
    loads = [(1 << 20) // math.isqrt(rank ** slope) + 1 for rank in range(1, amount + 1)]
    largest = bound if full else min(bound, max(-(-total // amount), total * loads[0] // sum(loads)))
    least = 1 if total - largest >= amount - 1 else 0
    counts, spare = [largest] + [least] * (amount - 1), total - largest - least * (amount - 1)
    while spare > 0:
        candidates = [i for i in range(1, amount) if counts[i] < largest] or [i for i in range(1, amount) if counts[i] < bound]
        mass, left = sum([loads[i] for i in candidates]), spare
        for i in candidates:
            addition = min(bound - counts[i], max(1, left * loads[i] // mass), spare)
            counts[i] = counts[i] + addition
            spare = spare - addition
    return np.array(counts)


def setup_inputs(seed: int = 0, part: int = 0) -> dict:
    arg_keys = jax.random.split(jax.random.key(seed), 12)
    part_keys = jax.random.split(jax.random.fold_in(arg_keys[11], part), 12)
    estimate = draw_estimate(jax.random.fold_in(jax.random.fold_in(arg_keys[11], part), 71), part)
    measured = draw_measured(jax.random.fold_in(jax.random.fold_in(arg_keys[11], part), 71), part)
    kernel_z = draw_kernel_z(jax.random.fold_in(arg_keys[11], 71), part)
    kernel_x = draw_kernel_x(jax.random.fold_in(arg_keys[11], 71), part)
    kernel_y = draw_kernel_y(jax.random.fold_in(arg_keys[11], 71), part)
    background = jnp.clip(jnp.exp(jax.random.uniform(arg_keys[5], (VIEWS,), jnp.float32, math.log(0.049804688), math.log(0.5))), 0.049804688, 0.5).astype(jnp.bfloat16)
    relax = jnp.clip(jnp.exp(jax.random.uniform(arg_keys[6], (VIEWS,), jnp.float32, math.log(0.029907227), math.log(0.23925781))), 0.029907227, 0.23925781).astype(jnp.bfloat16)
    owner_keys = jax.random.split(jax.random.fold_in(part_keys[7], 1), (BLOCKS * LIST) // LIST)
    owner_turns = jax.random.permutation(jax.random.fold_in(part_keys[7], 3), (BLOCKS * LIST) // LIST)
    owner = jax.vmap(lambda own, number: assign_block(jax.random.fold_in(part_keys[7], 2), own, number, LIST, BLOCKS, 1, CAP, 2))(owner_keys, owner_turns).reshape((BLOCKS * LIST, 1))
    source_offset = set_ends(jax.random.randint(part_keys[8], (BLOCKS * LIST,), 0, ROWS - SROWS + 1), jax.random.fold_in(part_keys[8], 1), 0, ROWS - SROWS).astype(jnp.int32)
    tile_offset = set_ends(jax.random.randint(part_keys[9], (BLOCKS * LIST,), 0, TROWS - SROWS + 1), jax.random.fold_in(part_keys[9], 1), 0, TROWS - SROWS).astype(jnp.int32)
    feather = set_ends(jax.random.randint(part_keys[10], (BLOCKS * LIST, SROWS), 1, 9), jax.random.fold_in(part_keys[10], 1), 1, 8).astype(jnp.int32)
    return dict(estimate=estimate, measured=measured, kernel_z=kernel_z, kernel_x=kernel_x, kernel_y=kernel_y, background=background, relax=relax, owner=owner, source_offset=source_offset, tile_offset=tile_offset, feather=feather)


smooth_rate = 0.24
edge_scale = 1.0


def kron_rows(kernel_x, kernel_y):
    outer = kernel_x.astype(jnp.float32)[..., :, None, :, None] * kernel_y.astype(jnp.float32)[..., None, :, None, :]
    rows_xy = kernel_x.shape[-1] * kernel_y.shape[-1]
    return outer.reshape(outer.shape[:-4] + (rows_xy, rows_xy)).astype(jnp.bfloat16)


def rounded(values):
    return lax.optimization_barrier(values.astype(jnp.bfloat16)).astype(jnp.float32)


def visit_view(block, kernel_z, kernel_xy, measured_block, back_value, relax_value):
    highest = lax.Precision.HIGHEST
    zeta = kernel_z.astype(jnp.float32)
    plane = kernel_xy.astype(jnp.float32)
    lowered = rounded(block)
    along_z = rounded(jnp.einsum("iz,rkz->rik", lowered, zeta, precision=highest))
    forward = jnp.einsum("rij,rjk->ik", plane, along_z, precision=highest)
    ratio_lo = rounded(measured_block.astype(jnp.float32) / (forward + back_value))
    back_z = rounded(jnp.einsum("ik,rkz->riz", ratio_lo, zeta, precision=highest))
    adjoint = jnp.einsum("rji,rjz->iz", plane, back_z, precision=highest)
    weights_sum = jnp.einsum("ri,rz->iz", jnp.sum(plane, axis=1), jnp.sum(zeta, axis=1), precision=highest)
    return block * jnp.exp(relax_value * jnp.log(adjoint / weights_sum))


def diffuse(volume):
    padded = jnp.pad(volume, 1)
    flux_sum = jnp.zeros_like(volume)
    for neighbor in (padded[2:, 1:-1], padded[:-2, 1:-1], padded[1:-1, 2:], padded[1:-1, :-2]):
        change = neighbor - volume
        flux_sum = flux_sum + change / (1.0 + (change / edge_scale) * (change / edge_scale))
    return volume + smooth_rate * flux_sum


def reference(estimate, measured, kernel_z, kernel_x, kernel_y, background, relax, owner, source_offset, tile_offset, feather):
    blocks = estimate.reshape(BLOCKS, ROWS, BZ)
    measured_all = measured.reshape(BLOCKS, VIEWS, ROWS, BZ)
    kernel_xy = kron_rows(kernel_x, kernel_y)
    back_values = background.astype(jnp.float32)
    relax_values = relax.astype(jnp.float32)

    def run_block(block_id, block):
        def advance(stop_id, carried):
            host_id = (block_id + stop_id) % BLOCKS
            view_id = host_id % VIEWS
            return visit_view(carried, kernel_z[view_id], kernel_xy[view_id], measured_all[host_id, stop_id], back_values[view_id], relax_values[view_id])
        return lax.fori_loop(0, VIEWS, advance, block)

    refined = jax.vmap(run_block)(jnp.arange(BLOCKS, dtype=jnp.int32), blocks).reshape(BLOCKS * ROWS, BZ)
    entries = jnp.arange(BLOCKS * LIST, dtype=jnp.int32)
    window_rows = jnp.arange(SROWS, dtype=jnp.int32)
    source_rows = ((entries // LIST) * ROWS + source_offset)[:, None] + window_rows[None, :]
    target_rows = (owner[:, 0] * TROWS + tile_offset)[:, None] + window_rows[None, :]
    weights = feather.astype(jnp.float32)
    pieces = refined[source_rows] * weights[..., None]
    numerator = 1.0 + jnp.zeros((BLOCKS * TROWS, BZ), jnp.float32).at[target_rows.reshape(-1)].add(pieces.reshape(-1, BZ))
    denominator = 1.0 + jnp.zeros((BLOCKS * TROWS,), jnp.float32).at[target_rows.reshape(-1)].add(weights.reshape(-1))
    joined = numerator / denominator[:, None]
    return refined, diffuse(joined)
```

```python
import functools

import jax
import jax.numpy as jnp
from jax import lax
from jax.experimental import pallas as pl
from jax.experimental.pallas import tpu as pltpu
from jax.sharding import PartitionSpec as P

SROWS = 8
TROWS = 64
CAP = 2
EDGE = CAP * SROWS
META = EDGE + 2
SLOT = 24
OFFSETS = CAP * SROWS
EDGE_WEIGHTS = OFFSETS + CAP

smooth_rate = 0.24
edge_scale = 1.0

f32 = jnp.float32
bf16 = jnp.bfloat16
VMEM = pl.BlockSpec(memory_space=pltpu.VMEM)
SMEM = pl.BlockSpec(memory_space=pltpu.SMEM)
ANY = pl.BlockSpec(memory_space=pl.ANY)


def dot(a, b):
    return jnp.dot(a, b, preferred_element_type=f32)


def by_target_kernel(place_ref, source_ref, target_ref, sems):
    count = target_ref.shape[0]
    copies = []
    for target in range(count):
        stop_id = lax.rem(place_ref[0] + count - target, count)
        copies.append(
            pltpu.make_async_copy(source_ref.at[stop_id], target_ref.at[target], sems.at[target])
        )
    for copy in copies:
        copy.start()
    for copy in copies:
        copy.wait()


def by_target(measured, place):
    return pl.pallas_call(
        by_target_kernel,
        out_shape=jax.ShapeDtypeStruct(measured.shape, measured.dtype),
        in_specs=[SMEM, ANY],
        out_specs=ANY,
        scratch_shapes=[pltpu.SemaphoreType.DMA((measured.shape[0],))],
    )(place, measured)


def prepare_kernel(
    x_ref, y_ref, back_x_ref, back_y_ref, spread_x_ref, spread_y_ref, z_ref, front_ref, back_ref, log_ref
):
    rank = z_ref.shape[1]
    for wide_x, wide_y, target_ref in (
        (x_ref, y_ref, front_ref),
        (back_x_ref, back_y_ref, back_ref),
    ):
        lines_x = dot(wide_x[0], spread_x_ref[...])
        lines_y = dot(wide_y[0], spread_y_ref[...])
        extent_y = lines_y.shape[0]
        for x in range(lines_x.shape[0]):
            target_ref[0, x * extent_y : (x + 1) * extent_y, :] = (
                lines_x[x : x + 1, :] * lines_y
            ).astype(bf16)
    lines = back_ref.shape[1]
    depth = z_ref.shape[3]
    ones = jnp.ones((lines, depth), bf16)
    total = jnp.zeros((lines, depth), f32)
    for r in range(rank):
        column_xy = dot(back_ref[0, :, r * lines : (r + 1) * lines], ones)
        column_z = jnp.sum(z_ref[0, r].astype(f32), axis=0, keepdims=True)
        total = total + column_xy * column_z
    log_ref[0] = jnp.log(total)


def prepare(kernel_x, kernel_y, kernel_z):
    views, rank, extent_x, _ = kernel_x.shape
    extent_y = kernel_y.shape[2]
    depth = kernel_z.shape[3]
    lines = extent_x * extent_y
    wide = rank * lines
    column = jnp.arange(wide, dtype=jnp.int32)
    part, inner = column // lines, column % lines
    rows_x = jnp.arange(rank * extent_x, dtype=jnp.int32)[:, None]
    rows_y = jnp.arange(rank * extent_y, dtype=jnp.int32)[:, None]
    spread_x = (rows_x == part * extent_x + inner // extent_y).astype(bf16)
    spread_y = (rows_y == part * extent_y + inner % extent_y).astype(bf16)
    front_x = kernel_x.transpose(0, 2, 1, 3).reshape(views, extent_x, rank * extent_x)
    front_y = kernel_y.transpose(0, 2, 1, 3).reshape(views, extent_y, rank * extent_y)
    back_x = kernel_x.transpose(0, 3, 1, 2).reshape(views, extent_x, rank * extent_x)
    back_y = kernel_y.transpose(0, 3, 1, 2).reshape(views, extent_y, rank * extent_y)

    def of_view(shape):
        return pl.BlockSpec((1,) + shape, lambda v: (v,) + (0,) * len(shape))

    def whole(array):
        return pl.BlockSpec(array.shape, lambda v: (0,) * array.ndim)

    return pl.pallas_call(
        prepare_kernel,
        grid=(views,),
        out_shape=(
            jax.ShapeDtypeStruct((views, lines, wide), bf16),
            jax.ShapeDtypeStruct((views, lines, wide), bf16),
            jax.ShapeDtypeStruct((views, lines, depth), f32),
        ),
        in_specs=[
            of_view(front_x.shape[1:]),
            of_view(front_y.shape[1:]),
            of_view(back_x.shape[1:]),
            of_view(back_y.shape[1:]),
            whole(spread_x),
            whole(spread_y),
            of_view(kernel_z.shape[1:]),
        ],
        out_specs=(of_view((lines, wide)), of_view((lines, wide)), of_view((lines, depth))),
        cost_estimate=pl.CostEstimate(
            flops=views * 8 * lines * wide, bytes_accessed=views * 8 * lines * wide, transcendentals=0
        ),
    )(front_x, front_y, back_x, back_y, spread_x, spread_y, kernel_z)


def stops_kernel(
    view_ref,
    record_ref,
    background_ref,
    relax_ref,
    slot_ref,
    owner_ref,
    source_ref,
    tile_ref,
    estimate_ref,
    weight_ref,
    meta_ref,
    front_hbm,
    back_hbm,
    toward_hbm,
    z_hbm,
    log_hbm,
    records_hbm,
    refined_ref,
    send_ref,
    front_ref,
    back_ref,
    toward_ref,
    z_ref,
    log_ref,
    records_ref,
    sems,
):
    stops = records_ref.shape[0]
    targets = send_ref.shape[0]
    rank = z_ref.shape[1] // z_ref.shape[2]
    depth = z_ref.shape[2]

    def copies(stop_id):
        view_id = view_ref[stop_id]
        pairs = (
            (toward_hbm.at[view_id], toward_ref),
            (front_hbm.at[view_id], front_ref),
            (records_hbm.at[record_ref[stop_id]], records_ref),
            (z_hbm.at[view_id], z_ref),
            (back_hbm.at[view_id], back_ref),
            (log_hbm.at[view_id], log_ref),
        )
        return [
            pltpu.make_async_copy(source, target.at[stop_id], sems.at[k, stop_id])
            for k, (source, target) in enumerate(pairs)
        ]

    ahead = min(2, stops)
    for stop_id in range(ahead):
        for copy in copies(stop_id):
            copy.start()

    def parts(factors, lines):
        return jnp.concatenate(
            [dot(lines, factors[r * depth : (r + 1) * depth]).astype(bf16) for r in range(rank)],
            axis=0,
        )

    def advance(stop_id, block):
        @pl.when(stop_id + ahead < stops)
        def _():
            for copy in copies(stop_id + ahead):
                copy.start()

        for copy in copies(stop_id):
            copy.wait()
        view_id = view_ref[stop_id]
        along_z = parts(toward_ref[stop_id], block.astype(bf16))
        forward = dot(front_ref[stop_id], along_z)
        ratio = (records_ref[stop_id].astype(f32) / (forward + background_ref[view_id])).astype(bf16)
        back_z = parts(z_ref[stop_id], ratio)
        adjoint = dot(back_ref[stop_id], back_z)
        return block * jnp.exp(relax_ref[view_id] * (jnp.log(adjoint) - log_ref[stop_id]))

    refined_ref[...] = lax.fori_loop(0, stops, advance, estimate_ref[...])

    send_ref[:, :EDGE, :] = jnp.zeros((targets, EDGE, depth), f32)
    send_ref[:, EDGE:, :] = meta_ref[...]

    def place(entry, carried):
        owner, tile = owner_ref[entry], tile_ref[entry]
        slot = slot_ref[entry]
        piece = refined_ref[pl.ds(source_ref[entry], SROWS), :] * weight_ref[entry]
        row = pl.multiple_of(lax.rem(slot, CAP) * SROWS, SROWS)
        send_ref[owner, pl.ds(row, SROWS), :] = piece

        @pl.when((tile == TROWS - SROWS) & (owner + 1 < targets))
        def _():
            send_ref[owner + 1, EDGE : EDGE + 1, :] += piece[SROWS - 1 :]

        @pl.when((tile == 0) & (owner > 0))
        def _():
            send_ref[owner - 1, EDGE + 1 : EDGE + 2, :] += piece[:1]

        return carried

    lax.fori_loop(0, source_ref.shape[0], place, 0)


def run_stops(scalars, estimate, weights, meta, front, back, toward, kernel_z, logs, records):
    lines, depth = estimate.shape
    stops = records.shape[0]
    targets = meta.shape[0]
    staged = (front, back, toward, kernel_z, logs, records)
    return pl.pallas_call(
        stops_kernel,
        out_shape=(
            jax.ShapeDtypeStruct((lines, depth), f32),
            jax.ShapeDtypeStruct((targets, SLOT, depth), f32),
        ),
        in_specs=[SMEM] * len(scalars) + [VMEM] * 3 + [ANY] * len(staged),
        out_specs=(VMEM, VMEM),
        scratch_shapes=[pltpu.VMEM((stops,) + a.shape[1:], a.dtype) for a in staged]
        + [pltpu.SemaphoreType.DMA((len(staged), stops))],
        compiler_params=pltpu.CompilerParams(vmem_limit_bytes=32 << 20),
    )(*scalars, estimate, weights, meta, *staged)


def blend_kernel(place_ref, data_ref, smoothed_ref):
    count, _, depth = data_ref.shape
    place = place_ref[0]
    slots = count * EDGE
    meta = data_ref[:, META, :]
    key = lax.broadcasted_iota(jnp.int32, (depth, slots), 0)
    column = lax.broadcasted_iota(jnp.int32, (depth, slots), 1) % EDGE
    spread_weight = (key == column).astype(bf16)
    spread_offset = (key == OFFSETS + column // SROWS).astype(bf16)
    own = lax.broadcasted_iota(jnp.int32, (count, slots), 0) == (
        lax.broadcasted_iota(jnp.int32, (count, slots), 1) // EDGE
    )
    coded = meta.astype(bf16)
    weight = jnp.sum(jnp.where(own, dot(coded, spread_weight), 0.0), axis=0, keepdims=True)
    offset = jnp.sum(jnp.where(own, dot(coded, spread_offset), 0.0), axis=0, keepdims=True)
    line = offset.astype(jnp.int32) + lax.broadcasted_iota(jnp.int32, (1, slots), 1) % SROWS
    placed = (line == lax.broadcasted_iota(jnp.int32, (TROWS, slots), 0)).astype(f32)
    data = data_ref[:, :EDGE, :].reshape(slots, depth)
    numerator = 1.0 + jnp.dot(
        placed, data, preferred_element_type=f32, precision=lax.Precision.HIGHEST
    )
    denominator = 1.0 + jnp.sum(placed * weight, axis=1, keepdims=True)
    joined = numerator / denominator

    def edge(which, inside):
        top = 1.0 + jnp.sum(data_ref[:, EDGE + which, :], axis=0, keepdims=True)
        lane = EDGE_WEIGHTS + which
        below = 1.0 + jnp.sum(meta[:, lane : lane + 1], axis=0, keepdims=True)
        return jnp.where(inside, top / below, 0.0)

    behind = edge(0, place > 0)
    beyond = edge(1, place < count - 1)
    side = jnp.zeros((TROWS, 1), f32)
    flux = jnp.zeros_like(joined)
    for neighbor in (
        jnp.concatenate([joined[1:], beyond], axis=0),
        jnp.concatenate([behind, joined[:-1]], axis=0),
        jnp.concatenate([joined[:, 1:], side], axis=1),
        jnp.concatenate([side, joined[:, :-1]], axis=1),
    ):
        change = neighbor - joined
        flux = flux + change / (1.0 + change / edge_scale * (change / edge_scale))
    smoothed_ref[...] = joined + smooth_rate * flux


def blend(place, data):
    return pl.pallas_call(
        blend_kernel,
        out_shape=jax.ShapeDtypeStruct((TROWS, data.shape[2]), f32),
        in_specs=[SMEM, VMEM],
        out_specs=VMEM,
        compiler_params=pltpu.CompilerParams(vmem_limit_bytes=32 << 20),
    )(place, data)


def listing(owner, tile_offset, feather, targets):
    listed = owner.shape[0]
    entry_ids = jnp.arange(listed, dtype=jnp.int32)
    earlier = (owner[:, None] == owner[None, :]) & (entry_ids[None, :] < entry_ids[:, None])
    slot_ids = owner * CAP + jnp.sum(earlier.astype(jnp.int32), axis=1)
    weights = feather.astype(f32)
    slots = jnp.arange(targets * CAP, dtype=jnp.int32)[:, None]
    taken = (slots == slot_ids[None, :]).astype(f32)
    slot_weights = jnp.sum(taken[:, :, None] * weights[None], axis=1).reshape(targets, CAP * SROWS)
    slot_offsets = jnp.sum(taken * tile_offset.astype(f32)[None], axis=1).reshape(targets, CAP)
    tiles = jnp.arange(targets, dtype=jnp.int32)[:, None]
    last = (owner[None] + 1 == tiles) & (tile_offset[None] == TROWS - SROWS)
    first = (owner[None] - 1 == tiles) & (tile_offset[None] == 0)
    edge_weights = [
        jnp.sum(jnp.where(reached, weights[None, :, q], 0.0), axis=1, keepdims=True)
        for reached, q in ((last, SROWS - 1), (first, 0))
    ]
    row = jnp.concatenate([slot_weights, slot_offsets] + edge_weights, axis=1)
    return slot_ids, weights, row


def on_device(
    estimate,
    measured,
    kernel_z,
    kernel_x,
    kernel_y,
    background,
    relax,
    owner,
    source_offset,
    tile_offset,
    feather,
):
    count = lax.axis_size("view")
    position = lax.axis_index("view").astype(jnp.int32)
    place = position.reshape(1)
    stops = measured.shape[0]
    views, rank, depth, _ = kernel_z.shape
    stop_ids = jnp.arange(stops, dtype=jnp.int32)
    hosts = (position + stop_ids) % count
    view_ids = hosts % views
    if stops == count:
        records = lax.all_to_all(
            by_target(measured, place), "view", split_axis=0, concat_axis=0, tiled=True
        )
        record_ids = hosts
    else:
        arrived = [measured[0]]
        for stop_id in range(1, stops):
            route = [((i + stop_id) % count, i) for i in range(count)]
            arrived.append(lax.ppermute(measured[stop_id], "view", route))
        records = jnp.stack(arrived, axis=0)
        record_ids = stop_ids

    front, back, logs = prepare(kernel_x, kernel_y, kernel_z)
    toward = kernel_z.swapaxes(2, 3).reshape(views, rank * depth, depth)
    owner = owner[:, 0]
    slot_ids, weights, row = listing(owner, tile_offset, feather, count)
    meta = jnp.zeros((count, SLOT - EDGE, depth), f32).at[:, META - EDGE, : row.shape[1]].set(row)
    weights = jnp.broadcast_to(weights[:, :, None], weights.shape + (depth,))
    scalars = (
        view_ids,
        record_ids,
        background.astype(f32),
        relax.astype(f32),
        slot_ids,
        owner,
        source_offset,
        tile_offset,
    )
    refined, outgoing = run_stops(
        scalars,
        estimate,
        weights,
        meta,
        front,
        back,
        toward,
        kernel_z.reshape(views, rank * depth, depth),
        logs,
        records,
    )
    incoming = lax.all_to_all(outgoing, "view", split_axis=0, concat_axis=0, tiled=True)
    return refined, blend(place, incoming)


def solution(mesh):
    lined = P(("groups", "view"))
    return jax.shard_map(
        on_device,
        mesh=mesh,
        in_specs=(
            P(("groups", "view"), None),
            P(("groups", "view"), None, None),
            P(),
            P(),
            P(),
            P(),
            P(),
            P(("groups", "view"), None),
            lined,
            lined,
            P(("groups", "view"), None),
        ),
        out_specs=(P(("groups", "view"), None), P(("groups", "view"), None)),
        check_vma=False,
    )
```

```python
import functools

import jax
import jax.numpy as jnp
from jax import lax
from jax.experimental import pallas as pl
from jax.experimental.pallas import tpu as pltpu
from jax.sharding import PartitionSpec as P

SROWS = 8
TROWS = 64
CAP = 2
EDGE = CAP * SROWS
META = EDGE + 2
SLOT = 24
OFFSETS = CAP * SROWS
EDGE_WEIGHTS = OFFSETS + CAP

smooth_rate = 0.24
edge_scale = 1.0

f32 = jnp.float32
bf16 = jnp.bfloat16
VMEM = pl.BlockSpec(memory_space=pltpu.VMEM)
SMEM = pl.BlockSpec(memory_space=pltpu.SMEM)


def dot(a, b):
    return jnp.dot(a, b, preferred_element_type=f32)


def spread_over(extent_x, extent_y, rank, of_x):
    extent = extent_x if of_x else extent_y
    shape = (rank * extent, rank * extent_x * extent_y)
    row = lax.broadcasted_iota(jnp.int32, shape, 0)
    column = lax.broadcasted_iota(jnp.int32, shape, 1)
    lines = extent_x * extent_y
    inner = column % lines
    inner = inner // extent_y if of_x else inner % extent_y
    return (row == column // lines * extent + inner).astype(bf16)


def prepare_kernel(
    x_ref, y_ref, back_x_ref, back_y_ref, z_ref, front_ref, back_ref, log_ref, lines_x_ref, lines_y_ref
):
    views, rank, _, depth = z_ref.shape
    extent_x = x_ref.shape[0] // views
    extent_y = y_ref.shape[0] // views
    lines = extent_x * extent_y
    spread_x = spread_over(extent_x, extent_y, rank, True)
    spread_y = spread_over(extent_x, extent_y, rank, False)
    for way, (wide_x_ref, wide_y_ref) in enumerate(((x_ref, y_ref), (back_x_ref, back_y_ref))):
        lines_x_ref[way] = dot(wide_x_ref[...], spread_x)
        lines_y_ref[way] = dot(wide_y_ref[...], spread_y)
    ones = jnp.ones((lines, depth), bf16)

    def of_view(view_id, carried):
        for way, target_ref in enumerate((front_ref, back_ref)):
            first = pl.multiple_of(view_id * extent_y, extent_y)
            lines_y = lines_y_ref[way, pl.ds(first, extent_y), :]
            for x in range(extent_x):
                line_x = lines_x_ref[way, pl.ds(x * views + view_id, 1), :]
                target_ref[view_id, x * extent_y : (x + 1) * extent_y, :] = (
                    line_x * lines_y
                ).astype(bf16)
        total = jnp.zeros((lines, depth), f32)
        for r in range(rank):
            column_xy = dot(back_ref[view_id, :, r * lines : (r + 1) * lines], ones)
            column_z = jnp.sum(z_ref[view_id, r].astype(f32), axis=0, keepdims=True)
            total = total + column_xy * column_z
        log_ref[view_id] = jnp.log(total)
        return carried

    lax.fori_loop(0, views, of_view, 0)


def prepare(kernel_x, kernel_y, kernel_z):
    views, rank, extent_x, _ = kernel_x.shape
    extent_y = kernel_y.shape[2]
    depth = kernel_z.shape[3]
    lines = extent_x * extent_y
    wide = rank * lines
    front_x = kernel_x.transpose(2, 0, 1, 3).reshape(extent_x * views, rank * extent_x)
    front_y = kernel_y.transpose(0, 2, 1, 3).reshape(views * extent_y, rank * extent_y)
    back_x = kernel_x.transpose(3, 0, 1, 2).reshape(extent_x * views, rank * extent_x)
    back_y = kernel_y.transpose(0, 3, 1, 2).reshape(views * extent_y, rank * extent_y)
    return pl.pallas_call(
        prepare_kernel,
        out_shape=(
            jax.ShapeDtypeStruct((views, lines, wide), bf16),
            jax.ShapeDtypeStruct((views, lines, wide), bf16),
            jax.ShapeDtypeStruct((views, lines, depth), f32),
        ),
        in_specs=[VMEM] * 5,
        out_specs=[VMEM] * 3,
        scratch_shapes=[
            pltpu.VMEM((2, extent_x * views, wide), f32),
            pltpu.VMEM((2, extent_y * views, wide), f32),
        ],
        compiler_params=pltpu.CompilerParams(vmem_limit_bytes=32 << 20),
        cost_estimate=pl.CostEstimate(
            flops=views * 8 * lines * wide, bytes_accessed=views * 8 * lines * wide, transcendentals=0
        ),
    )(front_x, front_y, back_x, back_y, kernel_z)


def stops_kernel(
    view_ref,
    record_ref,
    background_ref,
    relax_ref,
    slot_ref,
    owner_ref,
    source_ref,
    tile_ref,
    estimate_ref,
    weight_ref,
    meta_ref,
    front_ref,
    back_ref,
    toward_ref,
    z_ref,
    log_ref,
    records_ref,
    refined_ref,
    send_ref,
):
    stops = records_ref.shape[0]
    targets = send_ref.shape[0]
    rank = z_ref.shape[1] // z_ref.shape[2]
    depth = z_ref.shape[2]

    def parts(factors, lines):
        return jnp.concatenate(
            [dot(lines, factors[r * depth : (r + 1) * depth]).astype(bf16) for r in range(rank)],
            axis=0,
        )

    def advance(stop_id, block):
        view_id = view_ref[stop_id]
        record = records_ref[record_ref[stop_id]].astype(f32)
        along_z = parts(toward_ref[view_id], block.astype(bf16))
        forward = dot(front_ref[view_id], along_z)
        ratio = (record / (forward + background_ref[view_id])).astype(bf16)
        back_z = parts(z_ref[view_id], ratio)
        adjoint = dot(back_ref[view_id], back_z)
        return block * jnp.exp(relax_ref[view_id] * (jnp.log(adjoint) - log_ref[view_id]))

    refined_ref[...] = lax.fori_loop(0, stops, advance, estimate_ref[...])

    send_ref[:, :EDGE, :] = jnp.zeros((targets, EDGE, depth), f32)
    send_ref[:, EDGE:, :] = meta_ref[...]

    def place(entry, carried):
        owner, tile = owner_ref[entry], tile_ref[entry]
        slot = slot_ref[entry]
        piece = refined_ref[pl.ds(source_ref[entry], SROWS), :] * weight_ref[entry]
        row = pl.multiple_of(lax.rem(slot, CAP) * SROWS, SROWS)
        send_ref[owner, pl.ds(row, SROWS), :] = piece

        @pl.when((tile == TROWS - SROWS) & (owner + 1 < targets))
        def _():
            send_ref[owner + 1, EDGE : EDGE + 1, :] += piece[SROWS - 1 :]

        @pl.when((tile == 0) & (owner > 0))
        def _():
            send_ref[owner - 1, EDGE + 1 : EDGE + 2, :] += piece[:1]

        return carried

    lax.fori_loop(0, source_ref.shape[0], place, 0)


def run_stops(scalars, estimate, weights, meta, front, back, toward, kernel_z, logs, records):
    staged = (estimate, weights, meta, front, back, toward, kernel_z, logs, records)
    return pl.pallas_call(
        stops_kernel,
        out_shape=(
            jax.ShapeDtypeStruct(estimate.shape, f32),
            jax.ShapeDtypeStruct((meta.shape[0], SLOT, estimate.shape[1]), f32),
        ),
        in_specs=[SMEM] * len(scalars) + [VMEM] * len(staged),
        out_specs=(VMEM, VMEM),
        compiler_params=pltpu.CompilerParams(vmem_limit_bytes=32 << 20),
    )(*scalars, *staged)


def blend_kernel(place_ref, data_ref, smoothed_ref):
    count, _, depth = data_ref.shape
    place = place_ref[0]
    slots = count * EDGE
    meta = data_ref[:, META, :]
    key = lax.broadcasted_iota(jnp.int32, (depth, slots), 0)
    column = lax.broadcasted_iota(jnp.int32, (depth, slots), 1) % EDGE
    spread_weight = (key == column).astype(bf16)
    spread_offset = (key == OFFSETS + column // SROWS).astype(bf16)
    own = lax.broadcasted_iota(jnp.int32, (count, slots), 0) == (
        lax.broadcasted_iota(jnp.int32, (count, slots), 1) // EDGE
    )
    coded = meta.astype(bf16)
    weight = jnp.sum(jnp.where(own, dot(coded, spread_weight), 0.0), axis=0, keepdims=True)
    offset = jnp.sum(jnp.where(own, dot(coded, spread_offset), 0.0), axis=0, keepdims=True)
    line = offset.astype(jnp.int32) + lax.broadcasted_iota(jnp.int32, (1, slots), 1) % SROWS
    placed = (line == lax.broadcasted_iota(jnp.int32, (TROWS, slots), 0)).astype(f32)
    data = data_ref[:, :EDGE, :].reshape(slots, depth)
    numerator = 1.0 + jnp.dot(
        placed, data, preferred_element_type=f32, precision=lax.Precision.HIGHEST
    )
    denominator = 1.0 + jnp.sum(placed * weight, axis=1, keepdims=True)
    joined = numerator / denominator

    def edge(which, inside):
        top = 1.0 + jnp.sum(data_ref[:, EDGE + which, :], axis=0, keepdims=True)
        lane = EDGE_WEIGHTS + which
        below = 1.0 + jnp.sum(meta[:, lane : lane + 1], axis=0, keepdims=True)
        return jnp.where(inside, top / below, 0.0)

    behind = edge(0, place > 0)
    beyond = edge(1, place < count - 1)
    side = jnp.zeros((TROWS, 1), f32)
    flux = jnp.zeros_like(joined)
    for neighbor in (
        jnp.concatenate([joined[1:], beyond], axis=0),
        jnp.concatenate([behind, joined[:-1]], axis=0),
        jnp.concatenate([joined[:, 1:], side], axis=1),
        jnp.concatenate([side, joined[:, :-1]], axis=1),
    ):
        change = neighbor - joined
        flux = flux + change / (1.0 + change / edge_scale * (change / edge_scale))
    smoothed_ref[...] = joined + smooth_rate * flux


def blend(place, data):
    return pl.pallas_call(
        blend_kernel,
        out_shape=jax.ShapeDtypeStruct((TROWS, data.shape[2]), f32),
        in_specs=[SMEM, VMEM],
        out_specs=VMEM,
        compiler_params=pltpu.CompilerParams(vmem_limit_bytes=32 << 20),
    )(place, data)


def listing(owner, tile_offset, feather, targets):
    listed = owner.shape[0]
    entry_ids = jnp.arange(listed, dtype=jnp.int32)
    earlier = (owner[:, None] == owner[None, :]) & (entry_ids[None, :] < entry_ids[:, None])
    slot_ids = owner * CAP + jnp.sum(earlier.astype(jnp.int32), axis=1)
    weights = feather.astype(f32)
    slots = jnp.arange(targets * CAP, dtype=jnp.int32)[:, None]
    taken = (slots == slot_ids[None, :]).astype(f32)
    slot_weights = jnp.sum(taken[:, :, None] * weights[None], axis=1).reshape(targets, CAP * SROWS)
    slot_offsets = jnp.sum(taken * tile_offset.astype(f32)[None], axis=1).reshape(targets, CAP)
    tiles = jnp.arange(targets, dtype=jnp.int32)[:, None]
    last = (owner[None] + 1 == tiles) & (tile_offset[None] == TROWS - SROWS)
    first = (owner[None] - 1 == tiles) & (tile_offset[None] == 0)
    edge_weights = [
        jnp.sum(jnp.where(reached, weights[None, :, q], 0.0), axis=1, keepdims=True)
        for reached, q in ((last, SROWS - 1), (first, 0))
    ]
    row = jnp.concatenate([slot_weights, slot_offsets] + edge_weights, axis=1)
    return slot_ids, weights, row


def on_device(
    estimate,
    measured,
    kernel_z,
    kernel_x,
    kernel_y,
    background,
    relax,
    owner,
    source_offset,
    tile_offset,
    feather,
):
    count = lax.axis_size("view")
    position = lax.axis_index("view").astype(jnp.int32)
    place = position.reshape(1)
    stops = measured.shape[0]
    views, rank, depth, _ = kernel_z.shape
    stop_ids = jnp.arange(stops, dtype=jnp.int32)
    hosts = (position + stop_ids) % count
    view_ids = hosts % views
    if stops == count:
        by_target = measured[(position - stop_ids) % count]
        records = lax.all_to_all(by_target, "view", split_axis=0, concat_axis=0, tiled=True)
        record_ids = hosts
    else:
        arrived = [measured[0]]
        for stop_id in range(1, stops):
            route = [((i + stop_id) % count, i) for i in range(count)]
            arrived.append(lax.ppermute(measured[stop_id], "view", route))
        records = jnp.stack(arrived, axis=0)
        record_ids = stop_ids

    front, back, logs = prepare(kernel_x, kernel_y, kernel_z)
    toward = kernel_z.swapaxes(2, 3).reshape(views, rank * depth, depth)
    owner = owner[:, 0]
    slot_ids, weights, row = listing(owner, tile_offset, feather, count)
    meta = jnp.zeros((count, SLOT - EDGE, depth), f32).at[:, META - EDGE, : row.shape[1]].set(row)
    weights = jnp.broadcast_to(weights[:, :, None], weights.shape + (depth,))
    scalars = (
        view_ids,
        record_ids,
        background.astype(f32),
        relax.astype(f32),
        slot_ids,
        owner,
        source_offset,
        tile_offset,
    )
    refined, outgoing = run_stops(
        scalars,
        estimate,
        weights,
        meta,
        front,
        back,
        toward,
        kernel_z.reshape(views, rank * depth, depth),
        logs,
        records,
    )
    incoming = lax.all_to_all(outgoing, "view", split_axis=0, concat_axis=0, tiled=True)
    return refined, blend(place, incoming)


def solution(mesh):
    lined = P(("groups", "view"))
    return jax.shard_map(
        on_device,
        mesh=mesh,
        in_specs=(
            P(("groups", "view"), None),
            P(("groups", "view"), None, None),
            P(),
            P(),
            P(),
            P(),
            P(),
            P(("groups", "view"), None),
            lined,
            lined,
            P(("groups", "view"), None),
        ),
        out_specs=(P(("groups", "view"), None), P(("groups", "view"), None)),
        check_vma=False,
    )
```

```python
import functools

import jax
import jax.numpy as jnp
from jax import lax
from jax.experimental import pallas as pl
from jax.experimental.pallas import tpu as pltpu
from jax.sharding import PartitionSpec as P

SROWS = 8
TROWS = 64
CAP = 2
EDGE = CAP * SROWS
META = EDGE + 2
SLOT = 24
OFFSETS = CAP * SROWS
EDGE_WEIGHTS = OFFSETS + CAP

smooth_rate = 0.24
edge_scale = 1.0

f32 = jnp.float32
bf16 = jnp.bfloat16
VMEM = pl.BlockSpec(memory_space=pltpu.VMEM)
SMEM = pl.BlockSpec(memory_space=pltpu.SMEM)
ANY = pl.BlockSpec(memory_space=pl.ANY)
WHOLE = pltpu.CompilerParams(vmem_limit_bytes=60 << 20)


def dot(a, b, axis=0):
    return lax.dot_general(a, b, (((1,), (axis,)), ((), ())), preferred_element_type=f32)


def visit(block, record, planes_ref, logs, back_value, relax_value):
    lines, depth = block.shape
    rank = planes_ref.shape[1] // lines
    factors = [planes_ref[2 * lines :, r * depth : (r + 1) * depth] for r in range(rank)]
    lowered = block.astype(bf16)
    along_z = jnp.concatenate([dot(lowered, factor, 1).astype(bf16) for factor in factors], axis=0)
    forward = dot(planes_ref[:lines], along_z)
    ratio = (record.astype(f32) / (forward + back_value)).astype(bf16)
    back_z = jnp.concatenate([dot(ratio, factor).astype(bf16) for factor in factors], axis=0)
    adjoint = dot(planes_ref[lines : 2 * lines], back_z)
    return block * jnp.exp(relax_value * (jnp.log(adjoint) - logs))


def by_target_kernel(place_ref, source_ref, target_ref, held_ref, in_sems, out_sems):
    count = target_ref.shape[0]
    arrivals, departures = [], []
    for target in range(count):
        stop_id = lax.rem(place_ref[0] + count - target, count)
        arrivals.append(
            pltpu.make_async_copy(source_ref.at[stop_id], held_ref.at[target], in_sems.at[target])
        )
        departures.append(
            pltpu.make_async_copy(held_ref.at[target], target_ref.at[target], out_sems.at[target])
        )
    for arrival in arrivals:
        arrival.start()
    for arrival, departure in zip(arrivals, departures):
        arrival.wait()
        departure.start()
    for departure in departures:
        departure.wait()


def by_target(place, measured):
    count = measured.shape[0]
    return pl.pallas_call(
        by_target_kernel,
        out_shape=jax.ShapeDtypeStruct(measured.shape, measured.dtype),
        in_specs=[SMEM, ANY],
        out_specs=ANY,
        scratch_shapes=[
            pltpu.VMEM(measured.shape, measured.dtype),
            pltpu.SemaphoreType.DMA((count,)),
            pltpu.SemaphoreType.DMA((count,)),
        ],
        compiler_params=WHOLE,
    )(place, measured)


def make_planes(view_of, x_ref, y_ref, z_ref, planes_ref, log_ref, lines_x_ref, lines_y_ref, keep):
    views, rank, extent_y, _ = y_ref.shape
    extent_x = x_ref.shape[1]
    depth = z_ref.shape[2]
    lines = extent_x * extent_y
    wide = rank * lines

    def spread(extent, of_x, r):
        row = lax.broadcasted_iota(jnp.int32, (extent, wide), 0)
        column = lax.broadcasted_iota(jnp.int32, (extent, wide), 1) - r * lines
        inside = (column >= 0) & (column < lines)
        return (inside & (row == (column // extent_y if of_x else column % extent_y))).astype(bf16)

    rows = extent_x * views
    lines_x_ref[...] = sum(
        dot(x_ref[r * rows : (r + 1) * rows, :], spread(extent_x, True, r)) for r in range(rank)
    )
    lines_y_ref[...] = sum(
        dot(y_ref[:, r].reshape(views * extent_y, extent_y), spread(extent_y, False, r))
        for r in range(rank)
    )
    ones = jnp.ones((lines, depth), bf16)
    diagonal = (
        lax.broadcasted_iota(jnp.int32, (lines, lines), 0)
        == lax.broadcasted_iota(jnp.int32, (lines, lines), 1)
    ).astype(bf16)

    def of_stop(stop_id, carried):
        view_id = view_of(stop_id)
        first = pl.multiple_of(view_id * extent_y, extent_y)
        lines_y = lines_y_ref[pl.ds(first, extent_y), :]
        for x in range(extent_x):
            line_x = lines_x_ref[pl.ds(x * views + view_id, 1), :]
            planes_ref[stop_id, x * extent_y : (x + 1) * extent_y, :] = (
                line_x * lines_y
            ).astype(bf16)
        total = jnp.zeros((lines, depth), f32)
        turned = []
        for r in range(rank):
            plane = planes_ref[stop_id, :lines, r * lines : (r + 1) * lines]
            turned.append(dot(diagonal, plane, 1).astype(bf16))
            factor = z_ref[view_id, r * depth : (r + 1) * depth, :]
            planes_ref[stop_id, 2 * lines :, r * depth : (r + 1) * depth] = factor
            column_z = jnp.sum(factor.astype(f32), axis=0, keepdims=True)
            total = total + dot(turned[r], ones) * column_z
        planes_ref[stop_id, lines : 2 * lines, :] = jnp.concatenate(turned, axis=1)
        log_ref[stop_id] = jnp.log(total)
        for copy in keep(stop_id):
            copy.start()
        return carried

    lax.fori_loop(0, planes_ref.shape[0], of_stop, 0)


def clear(ref):
    def step(i, carried):
        ref[i] = 0
        return carried

    lax.fori_loop(0, ref.shape[0], step, 0)


def make_listing(owner_ref, tile_ref, feather_ref, weight_ref, meta_ref, codes_ref, taken_ref):
    listed = feather_ref.shape[0]
    depth = meta_ref.shape[1]
    targets = meta_ref.shape[0] // (SLOT - EDGE)
    feather = feather_ref[...].astype(f32).astype(bf16)
    key = lax.broadcasted_iota(jnp.int32, (SROWS, depth), 0)
    lane = lax.broadcasted_iota(jnp.int32, (SROWS, depth), 1)
    codes_ref[...] = dot(
        feather,
        (
            ((lane < OFFSETS) & (lane % SROWS == key))
            | ((lane == EDGE_WEIGHTS) & (key == SROWS - 1))
            | ((lane == EDGE_WEIGHTS + 1) & (key == 0))
        ).astype(bf16),
    )
    lines = listed * SROWS
    line = lax.broadcasted_iota(jnp.int32, (lines, listed), 0)
    chosen = (line // SROWS == lax.broadcasted_iota(jnp.int32, (lines, listed), 1)).astype(bf16)
    own = lax.broadcasted_iota(jnp.int32, (lines, SROWS), 1) == (
        lax.broadcasted_iota(jnp.int32, (lines, SROWS), 0) % SROWS
    )
    weight_ref[...] = dot(
        jnp.where(own, dot(chosen, feather), 0.0).astype(bf16), jnp.ones((SROWS, depth), bf16)
    )
    meta_ref[...] = jnp.zeros(meta_ref.shape, f32)
    at = META - EDGE
    lane = lax.broadcasted_iota(jnp.int32, (1, depth), 1)

    def add(target, row):
        meta_ref[pl.ds(target * (SLOT - EDGE) + at, 1), :] += row

    def enter(entry, carried):
        owner, tile = owner_ref[entry], tile_ref[entry]
        rank = taken_ref[owner]
        taken_ref[owner] = rank + 1
        code = codes_ref[pl.ds(entry, 1), :]
        own = (lane < OFFSETS) & (lane // SROWS == rank)
        offset = jnp.where(lane == OFFSETS + rank, tile.astype(f32), 0.0)
        add(owner, jnp.where(own, code, offset))

        @pl.when((tile == TROWS - SROWS) & (owner + 1 < targets))
        def _():
            add(owner + 1, jnp.where(lane == EDGE_WEIGHTS, code, 0.0))

        @pl.when((tile == 0) & (owner > 0))
        def _():
            add(owner - 1, jnp.where(lane == EDGE_WEIGHTS + 1, code, 0.0))

        return carried

    clear(taken_ref)
    lax.fori_loop(0, listed, enter, 0)


def rows_of(stops, lines, depth, listed, targets):
    lengths = (stops * lines, lines, listed * SROWS, targets * (SLOT - EDGE), listed, stops * SROWS)
    at = [0]
    for length in lengths:
        at.append(at[-1] + length)
    return at


def prepare_kernel(
    count,
    place_ref,
    values_ref,
    owner_ref,
    source_ref,
    tile_ref,
    estimate_ref,
    x_ref,
    y_ref,
    z_ref,
    feather_ref,
    measured_ref,
    planes_hbm,
    rows_hbm,
    planes_ref,
    log_ref,
    block_ref,
    weight_ref,
    meta_ref,
    places_ref,
    shares_ref,
    lines_x_ref,
    lines_y_ref,
    codes_ref,
    record_ref,
    taken_ref,
    sems,
    once_sems,
):
    stops, lines, depth = log_ref.shape
    rank = z_ref.shape[1] // depth
    copy = pltpu.make_async_copy(measured_ref.at[0], record_ref, once_sems.at[0])
    copy.start()

    def view_of(stop_id):
        return lax.rem(lax.rem(place_ref[0] + stop_id, count), z_ref.shape[0])

    def keep(stop_id):
        pairs = (
            (planes_ref.at[stop_id], planes_hbm.at[stop_id]),
            (
                log_ref.at[stop_id],
                rows_hbm.at[pl.ds(pl.multiple_of(stop_id * lines, SROWS), lines)],
            ),
        )
        return [
            pltpu.make_async_copy(source, target, sems.at[k, stop_id])
            for k, (source, target) in enumerate(pairs)
        ]

    key = lax.broadcasted_iota(jnp.int32, (1, depth), 1)

    def locate(entry, carried):
        row = jnp.where(key == 0, owner_ref[entry], tile_ref[entry])
        row = jnp.where(key == 1, source_ref[entry], row)
        places_ref[pl.ds(entry, 1), :] = row.astype(f32)
        return carried

    def share(stop_id, carried):
        view_id = view_of(stop_id)
        for k in range(2):
            shares_ref[pl.ds(stop_id * SROWS + k, 1), :] = jnp.full((1, depth), values_ref[k, view_id])
        return carried

    lax.fori_loop(0, owner_ref.shape[0], locate, 0)
    lax.fori_loop(0, stops, share, 0)
    make_planes(view_of, x_ref, y_ref, z_ref, planes_ref, log_ref, lines_x_ref, lines_y_ref, keep)
    make_listing(owner_ref, tile_ref, feather_ref, weight_ref, meta_ref, codes_ref, taken_ref)
    copy.wait()
    view_id = view_of(0)
    block_ref[...] = visit(
        estimate_ref[...],
        record_ref[...],
        planes_ref.at[0],
        log_ref[0],
        values_ref[0, view_id],
        values_ref[1, view_id],
    )
    at = rows_of(stops, lines, depth, owner_ref.shape[0], meta_ref.shape[0] // (SLOT - EDGE))
    finals = [
        pltpu.make_async_copy(ref, rows_hbm.at[pl.ds(first, ref.shape[0])], once_sems.at[k])
        for k, (ref, first) in enumerate(zip((block_ref, weight_ref, meta_ref, places_ref, shares_ref), at[1:]))
    ]
    for final in finals:
        final.start()

    def settle(stop_id, carried):
        for copy in keep(stop_id):
            copy.wait()
        return carried

    lax.fori_loop(0, stops, settle, 0)
    for final in finals:
        final.wait()


def prepare(count, scalars, estimate, kernel_x, kernel_y, kernel_z, feather, measured):
    views, rank, extent_x, _ = kernel_x.shape
    extent_y = kernel_y.shape[2]
    lines, depth = estimate.shape
    stops = measured.shape[0]
    wide = rank * lines
    listed = feather.shape[0]
    factors_x = kernel_x.transpose(1, 2, 0, 3).reshape(rank * extent_x * views, extent_x)
    planes = (stops, 2 * lines + depth, wide)
    rows = max(rows_of(stops, lines, depth, listed, count)[-1], 3 * stops * planes[1])
    return pl.pallas_call(
        functools.partial(prepare_kernel, count),
        out_shape=(jax.ShapeDtypeStruct(planes, bf16), jax.ShapeDtypeStruct((rows, depth), f32)),
        in_specs=[SMEM] * 5 + [VMEM] * 5 + [ANY],
        out_specs=[ANY] * 2,
        scratch_shapes=[
            pltpu.VMEM(planes, bf16),
            pltpu.VMEM((stops, lines, depth), f32),
            pltpu.VMEM((lines, depth), f32),
            pltpu.VMEM((listed * SROWS, depth), f32),
            pltpu.VMEM((count * (SLOT - EDGE), depth), f32),
            pltpu.VMEM((listed, depth), f32),
            pltpu.VMEM((stops * SROWS, depth), f32),
            pltpu.VMEM((extent_x * views, wide), f32),
            pltpu.VMEM((views * extent_y, wide), f32),
            pltpu.VMEM((listed, depth), f32),
            pltpu.VMEM((lines, depth), bf16),
            pltpu.SMEM((count,), jnp.int32),
            pltpu.SemaphoreType.DMA((2, stops)),
            pltpu.SemaphoreType.DMA((5,)),
        ],
        compiler_params=WHOLE,
        cost_estimate=pl.CostEstimate(
            flops=views * 8 * lines * wide, bytes_accessed=views * 8 * lines * wide, transcendentals=0
        ),
    )(*scalars, estimate, factors_x, kernel_y, kernel_z, feather, measured)


def stops_kernel(
    by_host,
    count,
    listed,
    place_ref,
    records_ref,
    planes_hbm,
    rows_hbm,
    refined_hbm,
    send_ref,
    planes_ref,
    log_ref,
    block_ref,
    weight_ref,
    shares_ref,
    places_ref,
    taken_ref,
    sems,
    once_sems,
):
    stops, lines, depth = log_ref.shape
    targets = send_ref.shape[0]
    at = rows_of(stops, lines, depth, listed, targets)

    groups = []
    first = 1
    while first < stops:
        groups.append((first, min(first, stops - first)))
        first += groups[-1][1]

    def arrivals(group):
        first, length = groups[group]
        copies = [
            pltpu.make_async_copy(
                planes_hbm.at[pl.ds(first, length)], planes_ref.at[pl.ds(first, length)], sems.at[0, group]
            )
        ]
        for stop_id in range(first, first + length):
            copies.append(
                pltpu.make_async_copy(
                    rows_hbm.at[pl.ds(stop_id * lines, lines)], log_ref.at[stop_id], sems.at[1, stop_id]
                )
            )
        return copies

    block_in, weights_in, places_in, shares_in = (
        pltpu.make_async_copy(rows_hbm.at[pl.ds(at[part], ref.shape[0])], ref, once_sems.at[k])
        for k, (part, ref) in enumerate(
            ((1, block_ref), (2, weight_ref), (4, places_ref), (5, shares_ref))
        )
    )
    metas_in = [
        pltpu.make_async_copy(
            rows_hbm.at[pl.ds(at[3] + target * (SLOT - EDGE), SLOT - EDGE)],
            send_ref.at[target, pl.ds(EDGE, SLOT - EDGE)],
            once_sems.at[5 + target],
        )
        for target in range(targets)
    ]
    block_in.start()
    shares_in.start()
    for group in range(len(groups)):
        for copy in arrivals(group):
            copy.start()
    weights_in.start()
    places_in.start()
    for copy in metas_in:
        copy.start()
    clear(taken_ref)
    send_ref[:, :EDGE, :] = jnp.zeros((targets, EDGE, depth), f32)
    block_in.wait()
    shares_in.wait()

    def advance(stop_id, block):
        for group, (first, _) in enumerate(groups):

            @pl.when(stop_id == first)
            def _(group=group):
                for copy in arrivals(group):
                    copy.wait()

        host = lax.rem(place_ref[0] + stop_id, count)
        shares = shares_ref[pl.ds(pl.multiple_of(stop_id * SROWS, SROWS), SROWS), :]
        return visit(
            block,
            records_ref[host if by_host else stop_id],
            planes_ref.at[stop_id],
            log_ref[stop_id],
            shares[:1],
            shares[1:2],
        )

    block_ref[...] = lax.fori_loop(1, stops, advance, block_ref[...])
    refined_out = pltpu.make_async_copy(block_ref, refined_hbm, once_sems.at[4])
    refined_out.start()
    weights_in.wait()
    places_in.wait()
    for copy in metas_in:
        copy.wait()

    def place(entry, carried):
        owner, source, tile = (places_ref[entry, k].astype(jnp.int32) for k in range(3))
        rank = taken_ref[owner]
        taken_ref[owner] = rank + 1
        weights = weight_ref[pl.ds(pl.multiple_of(entry * SROWS, SROWS), SROWS), :]
        piece = block_ref[pl.ds(source, SROWS), :] * weights
        send_ref[owner, pl.ds(pl.multiple_of(rank * SROWS, SROWS), SROWS), :] = piece

        @pl.when((tile == TROWS - SROWS) & (owner + 1 < targets))
        def _():
            send_ref[owner + 1, EDGE : EDGE + 1, :] += piece[SROWS - 1 :]

        @pl.when((tile == 0) & (owner > 0))
        def _():
            send_ref[owner - 1, EDGE + 1 : EDGE + 2, :] += piece[:1]

        return carried

    lax.fori_loop(0, listed, place, 0)
    refined_out.wait()


def run_stops(by_host, count, listed, place, records, planes, rows):
    stops, lines, depth = records.shape
    return pl.pallas_call(
        functools.partial(stops_kernel, by_host, count, listed),
        out_shape=(
            jax.ShapeDtypeStruct((lines, depth), f32),
            jax.ShapeDtypeStruct((count, SLOT, depth), f32),
        ),
        in_specs=[SMEM, VMEM, ANY, ANY],
        out_specs=(ANY, VMEM),
        scratch_shapes=[
            pltpu.VMEM(planes.shape, planes.dtype),
            pltpu.VMEM((stops, lines, depth), f32),
            pltpu.VMEM((lines, depth), f32),
            pltpu.VMEM((listed * SROWS, depth), f32),
            pltpu.VMEM((stops * SROWS, depth), f32),
            pltpu.SMEM((listed, depth), f32),
            pltpu.SMEM((count,), jnp.int32),
            pltpu.SemaphoreType.DMA((2, stops)),
            pltpu.SemaphoreType.DMA((5 + count,)),
        ],
        compiler_params=pltpu.CompilerParams(vmem_limit_bytes=51 << 20),
    )(place, records, planes, rows)


def blend_kernel(place_ref, data_ref, smoothed_ref):
    count, _, depth = data_ref.shape
    place = place_ref[0]
    slots = count * EDGE
    meta = data_ref[:, META, :]
    key = lax.broadcasted_iota(jnp.int32, (depth, slots), 0)
    column = lax.broadcasted_iota(jnp.int32, (depth, slots), 1) % EDGE
    spread_weight = (key == column).astype(bf16)
    spread_offset = (key == OFFSETS + column // SROWS).astype(bf16)
    own = lax.broadcasted_iota(jnp.int32, (count, slots), 0) == (
        lax.broadcasted_iota(jnp.int32, (count, slots), 1) // EDGE
    )
    coded = meta.astype(bf16)
    weight = jnp.sum(jnp.where(own, dot(coded, spread_weight), 0.0), axis=0, keepdims=True)
    offset = jnp.sum(jnp.where(own, dot(coded, spread_offset), 0.0), axis=0, keepdims=True)
    line = offset.astype(jnp.int32) + lax.broadcasted_iota(jnp.int32, (1, slots), 1) % SROWS
    placed = (line == lax.broadcasted_iota(jnp.int32, (TROWS, slots), 0)).astype(f32)
    data = data_ref[:, :EDGE, :].reshape(slots, depth)
    numerator = 1.0 + jnp.dot(
        placed, data, preferred_element_type=f32, precision=lax.Precision.HIGHEST
    )
    denominator = 1.0 + jnp.sum(placed * weight, axis=1, keepdims=True)
    joined = numerator / denominator

    def edge(which, inside):
        top = 1.0 + jnp.sum(data_ref[:, EDGE + which, :], axis=0, keepdims=True)
        lane = EDGE_WEIGHTS + which
        below = 1.0 + jnp.sum(meta[:, lane : lane + 1], axis=0, keepdims=True)
        return jnp.where(inside, top / below, 0.0)

    behind = edge(0, place > 0)
    beyond = edge(1, place < count - 1)
    side = jnp.zeros((TROWS, 1), f32)
    flux = jnp.zeros_like(joined)
    for neighbor in (
        jnp.concatenate([joined[1:], beyond], axis=0),
        jnp.concatenate([behind, joined[:-1]], axis=0),
        jnp.concatenate([joined[:, 1:], side], axis=1),
        jnp.concatenate([side, joined[:, :-1]], axis=1),
    ):
        change = neighbor - joined
        flux = flux + change / (1.0 + change / edge_scale * (change / edge_scale))
    smoothed_ref[...] = joined + smooth_rate * flux


def blend(place, data):
    return pl.pallas_call(
        blend_kernel,
        out_shape=jax.ShapeDtypeStruct((TROWS, data.shape[2]), f32),
        in_specs=[SMEM, VMEM],
        out_specs=VMEM,
        compiler_params=pltpu.CompilerParams(vmem_limit_bytes=32 << 20),
    )(place, data)


def on_device(
    estimate,
    measured,
    kernel_z,
    kernel_x,
    kernel_y,
    background,
    relax,
    owner,
    source_offset,
    tile_offset,
    feather,
):
    count = lax.axis_size("view")
    position = lax.axis_index("view").astype(jnp.int32)
    place = position.reshape(1)
    stops = measured.shape[0]
    views, rank, depth, _ = kernel_z.shape
    by_host = stops == count
    if by_host:
        records = lax.all_to_all(
            by_target(place, measured), "view", split_axis=0, concat_axis=0, tiled=True
        )
    else:
        arrived = [measured[0]]
        for stop_id in range(1, stops):
            route = [((i + stop_id) % count, i) for i in range(count)]
            arrived.append(lax.ppermute(measured[stop_id], "view", route))
        records = jnp.stack(arrived, axis=0)

    owner = owner[:, 0]
    values = jnp.stack([background, relax]).astype(f32)
    factors_z = kernel_z.reshape(views, rank * depth, depth)
    planes, rows = prepare(
        count,
        (place, values, owner, source_offset, tile_offset),
        estimate,
        kernel_x,
        kernel_y,
        factors_z,
        feather,
        measured,
    )
    refined, outgoing = run_stops(by_host, count, feather.shape[0], place, records, planes, rows)
    incoming = lax.all_to_all(outgoing, "view", split_axis=0, concat_axis=0, tiled=True)
    return refined, blend(place, incoming)


def solution(mesh):
    lined = P(("groups", "view"))
    return jax.shard_map(
        on_device,
        mesh=mesh,
        in_specs=(
            P(("groups", "view"), None),
            P(("groups", "view"), None, None),
            P(),
            P(),
            P(),
            P(),
            P(),
            P(("groups", "view"), None),
            lined,
            lined,
            P(("groups", "view"), None),
        ),
        out_specs=(P(("groups", "view"), None), P(("groups", "view"), None)),
        check_vma=False,
    )
```

```python
import functools

import jax
import jax.numpy as jnp
from jax import lax
from jax.experimental import pallas as pl
from jax.experimental.pallas import tpu as pltpu
from jax.sharding import PartitionSpec as P

SROWS = 8
TROWS = 64
CAP = 2
EDGE = CAP * SROWS
META = EDGE + 2
SLOT = 24
OFFSETS = CAP * SROWS
EDGE_WEIGHTS = OFFSETS + CAP

smooth_rate = 0.24
edge_scale = 1.0

f32 = jnp.float32
bf16 = jnp.bfloat16
VMEM = pl.BlockSpec(memory_space=pltpu.VMEM)
SMEM = pl.BlockSpec(memory_space=pltpu.SMEM)
ANY = pl.BlockSpec(memory_space=pl.ANY)
WHOLE = pltpu.CompilerParams(vmem_limit_bytes=60 << 20)


def dot(a, b, axis=0):
    return lax.dot_general(a, b, (((1,), (axis,)), ((), ())), preferred_element_type=f32)


def turned_dot(a, b):
    return lax.dot_general(a, b, (((0,), (0,)), ((), ())), preferred_element_type=f32)


def plane_rows(lines, depth):
    toward = (0, depth)
    front = (depth, lines)
    back_z = (depth + lines, depth)
    back = (2 * depth + lines, lines)
    return toward, front, back_z, back


def visit(block, record, planes_ref, log_ref, back_value, relax_value, ready=None):
    lines, depth = block.shape
    rank = planes_ref.shape[1] // lines

    def part(which):
        if ready is not None:
            ready(which)
        first, length = plane_rows(lines, depth)[which]
        return planes_ref[first : first + length, :]

    def along(rows, which):
        factors = part(which)
        parts = [dot(rows, factors[:, r * depth : (r + 1) * depth]).astype(bf16) for r in range(rank)]
        return jnp.concatenate(parts, axis=0)

    def across(which, stacked):
        plane = part(which)
        cut = 2 * depth
        return dot(plane[:, :cut], stacked[:cut]) + dot(plane[:, cut:], stacked[cut:])

    along_z = along(block.astype(bf16), 0)
    forward = across(1, along_z)
    ratio = (record.astype(f32) / (forward + back_value)).astype(bf16)
    back_z = along(ratio, 2)
    adjoint = across(3, back_z)
    if ready is not None:
        ready(4)
    return block * jnp.exp(relax_value * (jnp.log(adjoint) - log_ref[...]))


def by_target_kernel(source_ref, target_ref, held_ref, in_sems, out_sems):
    count = target_ref.shape[0]
    place = lax.axis_index("view")
    arrivals, departures = [], []
    for target in range(count):
        stop_id = lax.rem(place + count - target, count)
        arrivals.append(
            pltpu.make_async_copy(source_ref.at[stop_id], held_ref.at[target], in_sems.at[target])
        )
        departures.append(
            pltpu.make_async_copy(held_ref.at[target], target_ref.at[target], out_sems.at[target])
        )
    for arrival in arrivals:
        arrival.start()
    for arrival, departure in zip(arrivals, departures):
        arrival.wait()
        departure.start()
    for departure in departures:
        departure.wait()


def by_target(measured):
    count = measured.shape[0]
    return pl.pallas_call(
        by_target_kernel,
        out_shape=jax.ShapeDtypeStruct(measured.shape, measured.dtype),
        in_specs=[ANY],
        out_specs=ANY,
        scratch_shapes=[
            pltpu.VMEM(measured.shape, measured.dtype),
            pltpu.SemaphoreType.DMA((count,)),
            pltpu.SemaphoreType.DMA((count,)),
        ],
        compiler_params=WHOLE,
    )(measured)


def make_planes(view_of, x_ref, y_ref, z_ref, planes_ref, log_ref, lines_x_ref, lines_y_ref, keep):
    views, rank, extent_y, _ = y_ref.shape
    extent_x = x_ref.shape[1]
    depth = z_ref.shape[2]
    lines = extent_x * extent_y
    wide = rank * lines

    def spread(extent, of_x, r):
        row = lax.broadcasted_iota(jnp.int32, (extent, wide), 0)
        column = lax.broadcasted_iota(jnp.int32, (extent, wide), 1) - r * lines
        inside = (column >= 0) & (column < lines)
        return (inside & (row == (column // extent_y if of_x else column % extent_y))).astype(bf16)

    held = extent_x * views
    lines_x_ref[...] = sum(
        dot(x_ref[r * held : (r + 1) * held, :], spread(extent_x, True, r)) for r in range(rank)
    )
    lines_y_ref[...] = sum(
        dot(y_ref[:, r].reshape(views * extent_y, extent_y), spread(extent_y, False, r))
        for r in range(rank)
    )
    ones = jnp.ones((lines, depth), bf16)

    def diagonal(extent):
        row = lax.broadcasted_iota(jnp.int32, (extent, extent), 0)
        return (row == lax.broadcasted_iota(jnp.int32, (extent, extent), 1)).astype(bf16)

    toward, front, back_z, back = plane_rows(lines, depth)

    def rows(part):
        return slice(part[0], part[0] + part[1])

    def of_stop(stop_id, carried):
        view_id = view_of(stop_id)
        first = pl.multiple_of(view_id * extent_y, extent_y)
        lines_y = lines_y_ref[pl.ds(first, extent_y), :]
        for x in range(extent_x):
            line_x = lines_x_ref[pl.ds(x * views + view_id, 1), :]
            at = front[0] + x * extent_y
            planes_ref[stop_id, at : at + extent_y, :] = (line_x * lines_y).astype(bf16)
        total = jnp.zeros((lines, depth), f32)
        turned = []
        for r in range(rank):
            plane = planes_ref[stop_id, rows(front), r * lines : (r + 1) * lines]
            turned.append(dot(diagonal(lines), plane, 1).astype(bf16))
            factor = z_ref[view_id, r * depth : (r + 1) * depth, :]
            columns = slice(r * depth, (r + 1) * depth)
            planes_ref[stop_id, rows(back_z), columns] = factor
            planes_ref[stop_id, rows(toward), columns] = dot(diagonal(depth), factor, 1).astype(bf16)
            column_z = jnp.sum(factor.astype(f32), axis=0, keepdims=True)
            total = total + dot(turned[r], ones) * column_z
        planes_ref[stop_id, rows(back), :] = jnp.concatenate(turned, axis=1)
        log_ref[stop_id] = jnp.log(total)
        for copy in keep(stop_id):
            copy.start()
        return carried

    lax.fori_loop(0, planes_ref.shape[0], of_stop, 0)


def clear(ref):
    def step(i, carried):
        ref[i] = 0
        return carried

    lax.fori_loop(0, ref.shape[0], step, 0)


def make_listing(owner_ref, tile_ref, feather_ref, weight_ref, meta_ref, codes_ref, taken_ref):
    listed = feather_ref.shape[1]
    depth = meta_ref.shape[1]
    targets = meta_ref.shape[0] // (SLOT - EDGE)
    feather = feather_ref[...].astype(f32).astype(bf16)
    key = lax.broadcasted_iota(jnp.int32, (SROWS, depth), 0)
    lane = lax.broadcasted_iota(jnp.int32, (SROWS, depth), 1)
    codes_ref[...] = turned_dot(
        feather,
        (
            ((lane < OFFSETS) & (lane % SROWS == key))
            | ((lane == EDGE_WEIGHTS) & (key == SROWS - 1))
            | ((lane == EDGE_WEIGHTS + 1) & (key == 0))
        ).astype(bf16),
    )
    lines = listed * SROWS
    line = lax.broadcasted_iota(jnp.int32, (lines, listed), 0)
    chosen = (line // SROWS == lax.broadcasted_iota(jnp.int32, (lines, listed), 1)).astype(bf16)
    own = lax.broadcasted_iota(jnp.int32, (lines, SROWS), 1) == (
        lax.broadcasted_iota(jnp.int32, (lines, SROWS), 0) % SROWS
    )
    weight_ref[...] = dot(
        jnp.where(own, dot(chosen, feather, 1), 0.0).astype(bf16), jnp.ones((SROWS, depth), bf16)
    )
    meta_ref[...] = jnp.zeros(meta_ref.shape, f32)
    at = META - EDGE
    lane = lax.broadcasted_iota(jnp.int32, (1, depth), 1)

    def add(target, row):
        meta_ref[pl.ds(target * (SLOT - EDGE) + at, 1), :] += row

    def enter(entry, carried):
        owner, tile = owner_ref[entry], tile_ref[entry]
        rank = taken_ref[owner]
        taken_ref[owner] = rank + 1
        code = codes_ref[pl.ds(entry, 1), :]
        own = (lane < OFFSETS) & (lane // SROWS == rank)
        offset = jnp.where(lane == OFFSETS + rank, tile.astype(f32), 0.0)
        add(owner, jnp.where(own, code, offset))

        @pl.when((tile == TROWS - SROWS) & (owner + 1 < targets))
        def _():
            add(owner + 1, jnp.where(lane == EDGE_WEIGHTS, code, 0.0))

        @pl.when((tile == 0) & (owner > 0))
        def _():
            add(owner - 1, jnp.where(lane == EDGE_WEIGHTS + 1, code, 0.0))

        return carried

    clear(taken_ref)
    lax.fori_loop(0, listed, enter, 0)


def rows_of(stops, lines, depth, listed, targets):
    lengths = (stops * lines, lines, listed * SROWS, targets * (SLOT - EDGE), listed, stops * SROWS)
    at = [0]
    for length in lengths:
        at.append(at[-1] + length)
    return at


def prepare_kernel(
    count,
    owner_ref,
    source_ref,
    tile_ref,
    background_ref,
    relax_ref,
    estimate_ref,
    x_ref,
    y_ref,
    z_ref,
    feather_ref,
    measured_ref,
    planes_hbm,
    rows_hbm,
    planes_ref,
    log_ref,
    block_ref,
    weight_ref,
    meta_ref,
    places_ref,
    shares_ref,
    lines_x_ref,
    lines_y_ref,
    codes_ref,
    record_ref,
    taken_ref,
    sems,
    once_sems,
):
    stops, lines, depth = log_ref.shape
    rank = z_ref.shape[1] // depth
    copy = pltpu.make_async_copy(measured_ref.at[0], record_ref, once_sems.at[0])
    copy.start()

    place = lax.axis_index("view")

    def view_of(stop_id):
        return lax.rem(lax.rem(place + stop_id, count), z_ref.shape[0])

    def keep(stop_id):
        pairs = (
            (planes_ref.at[stop_id], planes_hbm.at[stop_id]),
            (
                log_ref.at[stop_id],
                rows_hbm.at[pl.ds(pl.multiple_of(stop_id * lines, SROWS), lines)],
            ),
        )
        return [
            pltpu.make_async_copy(source, target, sems.at[k, stop_id])
            for k, (source, target) in enumerate(pairs)
        ]

    key = lax.broadcasted_iota(jnp.int32, (1, depth), 1)

    def locate(entry, carried):
        row = jnp.where(key == 0, owner_ref[entry], tile_ref[entry])
        row = jnp.where(key == 1, source_ref[entry], row)
        places_ref[pl.ds(entry, 1), :] = row.astype(f32)
        return carried

    def share(stop_id, carried):
        own = lax.broadcasted_iota(jnp.int32, background_ref.shape, 1) == view_of(stop_id)
        for k, ref in enumerate((background_ref, relax_ref)):
            value = jnp.sum(jnp.where(own, ref[...].astype(f32), 0.0), axis=1, keepdims=True)
            shares_ref[pl.ds(stop_id * SROWS + k, 1), :] = jnp.broadcast_to(value, (1, depth))
        return carried

    lax.fori_loop(0, owner_ref.shape[0], locate, 0)
    lax.fori_loop(0, stops, share, 0)
    make_planes(view_of, x_ref, y_ref, z_ref, planes_ref, log_ref, lines_x_ref, lines_y_ref, keep)
    make_listing(owner_ref, tile_ref, feather_ref, weight_ref, meta_ref, codes_ref, taken_ref)
    copy.wait()
    block_ref[...] = visit(
        estimate_ref[...],
        record_ref[...],
        planes_ref.at[0],
        log_ref.at[0],
        shares_ref[:1],
        shares_ref[1:2],
    )
    at = rows_of(stops, lines, depth, owner_ref.shape[0], meta_ref.shape[0] // (SLOT - EDGE))
    finals = [
        pltpu.make_async_copy(ref, rows_hbm.at[pl.ds(first, ref.shape[0])], once_sems.at[k])
        for k, (ref, first) in enumerate(zip((block_ref, weight_ref, meta_ref, places_ref, shares_ref), at[1:]))
    ]
    for final in finals:
        final.start()

    def settle(stop_id, carried):
        for copy in keep(stop_id):
            copy.wait()
        return carried

    lax.fori_loop(0, stops, settle, 0)
    for final in finals:
        final.wait()


def prepare(count, listing, background, relax, estimate, kernel_x, kernel_y, kernel_z, feather, measured):
    views, rank, extent_x, _ = kernel_x.shape
    extent_y = kernel_y.shape[2]
    lines, depth = estimate.shape
    stops = measured.shape[0]
    wide = rank * lines
    listed = feather.shape[1]
    factors_x = kernel_x.transpose(1, 2, 0, 3).reshape(rank * extent_x * views, extent_x)
    planes = (stops, 2 * lines + 2 * depth, wide)
    rows = max(rows_of(stops, lines, depth, listed, count)[-1], 3 * stops * planes[1])
    return pl.pallas_call(
        functools.partial(prepare_kernel, count),
        out_shape=(jax.ShapeDtypeStruct(planes, bf16), jax.ShapeDtypeStruct((rows, depth), f32)),
        in_specs=[SMEM] * 3 + [VMEM] * 7 + [ANY],
        out_specs=[ANY] * 2,
        scratch_shapes=[
            pltpu.VMEM(planes, bf16),
            pltpu.VMEM((stops, lines, depth), f32),
            pltpu.VMEM((lines, depth), f32),
            pltpu.VMEM((listed * SROWS, depth), f32),
            pltpu.VMEM((count * (SLOT - EDGE), depth), f32),
            pltpu.VMEM((listed, depth), f32),
            pltpu.VMEM((stops * SROWS, depth), f32),
            pltpu.VMEM((extent_x * views, wide), f32),
            pltpu.VMEM((views * extent_y, wide), f32),
            pltpu.VMEM((listed, depth), f32),
            pltpu.VMEM((lines, depth), bf16),
            pltpu.SMEM((count,), jnp.int32),
            pltpu.SemaphoreType.DMA((2, stops)),
            pltpu.SemaphoreType.DMA((5,)),
        ],
        compiler_params=WHOLE,
        cost_estimate=pl.CostEstimate(
            flops=views * 8 * lines * wide, bytes_accessed=views * 8 * lines * wide, transcendentals=0
        ),
    )(*listing, background, relax, estimate, factors_x, kernel_y, kernel_z, feather, measured)


def stops_kernel(
    by_host,
    count,
    listed,
    records_ref,
    planes_hbm,
    rows_hbm,
    refined_hbm,
    send_ref,
    planes_ref,
    log_ref,
    block_ref,
    weight_ref,
    shares_ref,
    places_ref,
    taken_ref,
    sems,
    first_sems,
    once_sems,
):
    stops, lines, depth = log_ref.shape
    targets = send_ref.shape[0]
    at = rows_of(stops, lines, depth, listed, targets)
    position = lax.axis_index("view")

    groups = [(1, 1)]
    while sum(groups[-1]) < stops:
        first = sum(groups[-1])
        groups.append((first, min(first, stops - first)))

    def log_in(stop_id):
        return pltpu.make_async_copy(
            rows_hbm.at[pl.ds(stop_id * lines, lines)], log_ref.at[stop_id], sems.at[1, stop_id]
        )

    def arrivals(group):
        first, length = groups[group]
        if group == 0:
            copies = [
                pltpu.make_async_copy(
                    planes_hbm.at[first, pl.ds(*part)], planes_ref.at[first, pl.ds(*part)], first_sems.at[k]
                )
                for k, part in enumerate(plane_rows(lines, depth))
            ]
        else:
            copies = [
                pltpu.make_async_copy(
                    planes_hbm.at[pl.ds(first, length)],
                    planes_ref.at[pl.ds(first, length)],
                    sems.at[0, group],
                )
            ]
        return copies + [log_in(stop_id) for stop_id in range(first, first + length)]

    block_in, weights_in, places_in, shares_in = (
        pltpu.make_async_copy(rows_hbm.at[pl.ds(at[part], ref.shape[0])], ref, once_sems.at[k])
        for k, (part, ref) in enumerate(
            ((1, block_ref), (2, weight_ref), (4, places_ref), (5, shares_ref))
        )
    )
    metas_in = [
        pltpu.make_async_copy(
            rows_hbm.at[pl.ds(at[3] + target * (SLOT - EDGE), SLOT - EDGE)],
            send_ref.at[target, pl.ds(EDGE, SLOT - EDGE)],
            once_sems.at[5 + target],
        )
        for target in range(targets)
    ]
    block_in.start()
    shares_in.start()
    for group in range(len(groups)):
        for copy in arrivals(group):
            copy.start()
    weights_in.start()
    places_in.start()
    for copy in metas_in:
        copy.start()
    clear(taken_ref)
    send_ref[:, :EDGE, :] = jnp.zeros((targets, EDGE, depth), f32)
    block_in.wait()
    shares_in.wait()

    def advance(stop_id, block, ready=None):
        host = lax.rem(position + stop_id, count)
        shares = shares_ref[pl.ds(pl.multiple_of(stop_id * SROWS, SROWS), SROWS), :]
        return visit(
            block,
            records_ref[host if by_host else stop_id],
            planes_ref.at[stop_id],
            log_ref.at[stop_id],
            shares[:1],
            shares[1:2],
            ready,
        )

    first_copies = arrivals(0)
    block = advance(1, block_ref[...], lambda which: first_copies[which].wait())
    for group, (first, length) in enumerate(groups[1:], 1):
        for copy in arrivals(group):
            copy.wait()
        for stop_id in range(first, first + length):
            block = advance(stop_id, block)
    block_ref[...] = block
    refined_out = pltpu.make_async_copy(block_ref, refined_hbm, once_sems.at[4])
    refined_out.start()
    weights_in.wait()
    places_in.wait()
    for copy in metas_in:
        copy.wait()

    def place(entry, carried):
        owner, source, tile = (places_ref[entry, k].astype(jnp.int32) for k in range(3))
        rank = taken_ref[owner]
        taken_ref[owner] = rank + 1
        weights = weight_ref[pl.ds(pl.multiple_of(entry * SROWS, SROWS), SROWS), :]
        piece = block_ref[pl.ds(source, SROWS), :] * weights
        send_ref[owner, pl.ds(pl.multiple_of(rank * SROWS, SROWS), SROWS), :] = piece

        @pl.when((tile == TROWS - SROWS) & (owner + 1 < targets))
        def _():
            send_ref[owner + 1, EDGE : EDGE + 1, :] += piece[SROWS - 1 :]

        @pl.when((tile == 0) & (owner > 0))
        def _():
            send_ref[owner - 1, EDGE + 1 : EDGE + 2, :] += piece[:1]

        return carried

    lax.fori_loop(0, listed, place, 0)
    refined_out.wait()


def run_stops(by_host, count, listed, records, planes, rows):
    stops, lines, depth = records.shape
    return pl.pallas_call(
        functools.partial(stops_kernel, by_host, count, listed),
        out_shape=(
            jax.ShapeDtypeStruct((lines, depth), f32),
            jax.ShapeDtypeStruct((count, SLOT, depth), f32),
        ),
        in_specs=[VMEM, ANY, ANY],
        out_specs=(ANY, VMEM),
        scratch_shapes=[
            pltpu.VMEM(planes.shape, planes.dtype),
            pltpu.VMEM((stops, lines, depth), f32),
            pltpu.VMEM((lines, depth), f32),
            pltpu.VMEM((listed * SROWS, depth), f32),
            pltpu.VMEM((stops * SROWS, depth), f32),
            pltpu.SMEM((listed, depth), f32),
            pltpu.SMEM((count,), jnp.int32),
            pltpu.SemaphoreType.DMA((2, stops)),
            pltpu.SemaphoreType.DMA((4,)),
            pltpu.SemaphoreType.DMA((5 + count,)),
        ],
        compiler_params=pltpu.CompilerParams(vmem_limit_bytes=51 << 20),
    )(records, planes, rows)


def blend_kernel(data_ref, smoothed_ref):
    count, _, depth = data_ref.shape
    place = lax.axis_index("view")
    slots = count * EDGE
    meta = data_ref[:, META, :]
    key = lax.broadcasted_iota(jnp.int32, (depth, slots), 0)
    column = lax.broadcasted_iota(jnp.int32, (depth, slots), 1) % EDGE
    spread_weight = (key == column).astype(bf16)
    spread_offset = (key == OFFSETS + column // SROWS).astype(bf16)
    own = lax.broadcasted_iota(jnp.int32, (count, slots), 0) == (
        lax.broadcasted_iota(jnp.int32, (count, slots), 1) // EDGE
    )
    coded = meta.astype(bf16)
    weight = jnp.sum(jnp.where(own, dot(coded, spread_weight), 0.0), axis=0, keepdims=True)
    offset = jnp.sum(jnp.where(own, dot(coded, spread_offset), 0.0), axis=0, keepdims=True)
    line = offset.astype(jnp.int32) + lax.broadcasted_iota(jnp.int32, (1, slots), 1) % SROWS
    placed = (line == lax.broadcasted_iota(jnp.int32, (TROWS, slots), 0)).astype(f32)
    data = data_ref[:, :EDGE, :].reshape(slots, depth)
    numerator = 1.0 + jnp.dot(
        placed, data, preferred_element_type=f32, precision=lax.Precision.HIGHEST
    )
    denominator = 1.0 + jnp.sum(placed * weight, axis=1, keepdims=True)
    joined = numerator / denominator

    def edge(which, inside):
        top = 1.0 + jnp.sum(data_ref[:, EDGE + which, :], axis=0, keepdims=True)
        lane = EDGE_WEIGHTS + which
        below = 1.0 + jnp.sum(meta[:, lane : lane + 1], axis=0, keepdims=True)
        return jnp.where(inside, top / below, 0.0)

    behind = edge(0, place > 0)
    beyond = edge(1, place < count - 1)
    side = jnp.zeros((TROWS, 1), f32)
    flux = jnp.zeros_like(joined)
    for neighbor in (
        jnp.concatenate([joined[1:], beyond], axis=0),
        jnp.concatenate([behind, joined[:-1]], axis=0),
        jnp.concatenate([joined[:, 1:], side], axis=1),
        jnp.concatenate([side, joined[:, :-1]], axis=1),
    ):
        change = neighbor - joined
        flux = flux + change / (1.0 + change / edge_scale * (change / edge_scale))
    smoothed_ref[...] = joined + smooth_rate * flux


def blend(data):
    return pl.pallas_call(
        blend_kernel,
        out_shape=jax.ShapeDtypeStruct((TROWS, data.shape[2]), f32),
        in_specs=[VMEM],
        out_specs=VMEM,
        compiler_params=pltpu.CompilerParams(vmem_limit_bytes=32 << 20),
    )(data)


def on_device(
    estimate,
    measured,
    kernel_z,
    kernel_x,
    kernel_y,
    background,
    relax,
    owner,
    source_offset,
    tile_offset,
    feather,
):
    count = lax.axis_size("view")
    stops = measured.shape[0]
    views, rank, depth, _ = kernel_z.shape
    by_host = stops == count
    if by_host:
        records = lax.all_to_all(
            by_target(measured), "view", split_axis=0, concat_axis=0, tiled=True
        )
    else:
        arrived = [measured[0]]
        for stop_id in range(1, stops):
            route = [((i + stop_id) % count, i) for i in range(count)]
            arrived.append(lax.ppermute(measured[stop_id], "view", route))
        records = jnp.stack(arrived, axis=0)

    factors_z = kernel_z.reshape(views, rank * depth, depth)
    planes, rows = prepare(
        count,
        (owner[:, 0], source_offset, tile_offset),
        background[None],
        relax[None],
        estimate,
        kernel_x,
        kernel_y,
        factors_z,
        feather.T,
        measured,
    )
    refined, outgoing = run_stops(by_host, count, feather.shape[0], records, planes, rows)
    incoming = lax.all_to_all(outgoing, "view", split_axis=0, concat_axis=0, tiled=True)
    return refined, blend(incoming)


def solution(mesh):
    lined = P(("groups", "view"))
    return jax.shard_map(
        on_device,
        mesh=mesh,
        in_specs=(
            P(("groups", "view"), None),
            P(("groups", "view"), None, None),
            P(),
            P(),
            P(),
            P(),
            P(),
            P(("groups", "view"), None),
            lined,
            lined,
            P(("groups", "view"), None),
        ),
        out_specs=(P(("groups", "view"), None), P(("groups", "view"), None)),
        check_vma=False,
    )
```

```python
import functools

import jax
import jax.numpy as jnp
from jax import lax
from jax.experimental import pallas as pl
from jax.experimental.pallas import tpu as pltpu
from jax.sharding import PartitionSpec as P

SROWS = 8
TROWS = 64
CAP = 2
EDGE = CAP * SROWS
META = EDGE + 2
SLOT = 24
OFFSETS = CAP * SROWS
EDGE_WEIGHTS = OFFSETS + CAP

smooth_rate = 0.24
edge_scale = 1.0

f32 = jnp.float32
bf16 = jnp.bfloat16
VMEM = pl.BlockSpec(memory_space=pltpu.VMEM)
SMEM = pl.BlockSpec(memory_space=pltpu.SMEM)
ANY = pl.BlockSpec(memory_space=pl.ANY)
NEAR = pltpu.CompilerParams(vmem_limit_bytes=51 << 20)
WHOLE = pltpu.CompilerParams(vmem_limit_bytes=60 << 20)


def dot(a, b, axis=0):
    return lax.dot_general(a, b, (((1,), (axis,)), ((), ())), preferred_element_type=f32)


def turned_dot(a, b):
    return lax.dot_general(a, b, (((0,), (0,)), ((), ())), preferred_element_type=f32)


def plane_rows(lines, depth):
    toward = (0, depth)
    front = (depth, lines)
    back_z = (depth + lines, depth)
    back = (2 * depth + lines, lines)
    return toward, front, back_z, back


def visit(block, record, planes_ref, log_ref, back_value, relax_value, ready=None):
    lines, depth = block.shape
    rank = planes_ref.shape[1] // lines

    def part(which):
        if ready is not None:
            ready(which)
        first, length = plane_rows(lines, depth)[which]
        return planes_ref[first : first + length, :]

    def along(rows, which):
        factors = part(which)
        parts = [dot(rows, factors[:, r * depth : (r + 1) * depth]).astype(bf16) for r in range(rank)]
        return jnp.concatenate(parts, axis=0)

    def across(which, stacked):
        plane = part(which)
        cut = 2 * depth
        return dot(plane[:, :cut], stacked[:cut]) + dot(plane[:, cut:], stacked[cut:])

    along_z = along(block.astype(bf16), 0)
    forward = across(1, along_z)
    ratio = (record.astype(f32) / (forward + back_value)).astype(bf16)
    back_z = along(ratio, 2)
    adjoint = across(3, back_z)
    if ready is not None:
        ready(4)
    return block * jnp.exp(relax_value * (jnp.log(adjoint) - log_ref[...]))


def by_target_kernel(source_ref, target_ref, held_ref, in_sems, out_sems):
    count = target_ref.shape[0]
    place = lax.axis_index("view")
    arrivals, departures = [], []
    for target in range(count):
        stop_id = lax.rem(place + count - target, count)
        arrivals.append(
            pltpu.make_async_copy(source_ref.at[stop_id], held_ref.at[target], in_sems.at[target])
        )
        departures.append(
            pltpu.make_async_copy(held_ref.at[target], target_ref.at[target], out_sems.at[target])
        )
    for arrival in arrivals:
        arrival.start()
    for arrival, departure in zip(arrivals, departures):
        arrival.wait()
        departure.start()
    for departure in departures:
        departure.wait()


def by_target(measured):
    count = measured.shape[0]
    return pl.pallas_call(
        by_target_kernel,
        out_shape=jax.ShapeDtypeStruct(measured.shape, measured.dtype),
        in_specs=[ANY],
        out_specs=ANY,
        scratch_shapes=[
            pltpu.VMEM(measured.shape, measured.dtype),
            pltpu.SemaphoreType.DMA((count,)),
            pltpu.SemaphoreType.DMA((count,)),
        ],
        compiler_params=WHOLE,
    )(measured)


def make_planes(view_of, x_ref, y_ref, z_ref, planes_ref, log_ref, lines_x_ref, lines_y_ref, keep):
    views, rank, extent_y, _ = y_ref.shape
    extent_x = x_ref.shape[1]
    depth = z_ref.shape[2]
    lines = extent_x * extent_y
    wide = rank * lines

    def spread(extent, of_x, r):
        row = lax.broadcasted_iota(jnp.int32, (extent, wide), 0)
        column = lax.broadcasted_iota(jnp.int32, (extent, wide), 1) - r * lines
        inside = (column >= 0) & (column < lines)
        return (inside & (row == (column // extent_y if of_x else column % extent_y))).astype(bf16)

    held = extent_x * views
    lines_x_ref[...] = sum(
        dot(x_ref[r * held : (r + 1) * held, :], spread(extent_x, True, r)) for r in range(rank)
    )
    lines_y_ref[...] = sum(
        dot(y_ref[:, r].reshape(views * extent_y, extent_y), spread(extent_y, False, r))
        for r in range(rank)
    )
    ones = jnp.ones((lines, depth), bf16)

    def diagonal(extent):
        row = lax.broadcasted_iota(jnp.int32, (extent, extent), 0)
        return (row == lax.broadcasted_iota(jnp.int32, (extent, extent), 1)).astype(bf16)

    toward, front, back_z, back = plane_rows(lines, depth)

    def rows(part):
        return slice(part[0], part[0] + part[1])

    def of_stop(stop_id, carried):
        view_id = view_of(stop_id)
        first = pl.multiple_of(view_id * extent_y, extent_y)
        lines_y = lines_y_ref[pl.ds(first, extent_y), :]
        for x in range(extent_x):
            line_x = lines_x_ref[pl.ds(x * views + view_id, 1), :]
            at = front[0] + x * extent_y
            planes_ref[stop_id, at : at + extent_y, :] = (line_x * lines_y).astype(bf16)
        total = jnp.zeros((lines, depth), f32)
        turned = []
        for r in range(rank):
            plane = planes_ref[stop_id, rows(front), r * lines : (r + 1) * lines]
            turned.append(dot(diagonal(lines), plane, 1).astype(bf16))
            factor = z_ref[view_id, r * depth : (r + 1) * depth, :]
            columns = slice(r * depth, (r + 1) * depth)
            planes_ref[stop_id, rows(back_z), columns] = factor
            planes_ref[stop_id, rows(toward), columns] = dot(diagonal(depth), factor, 1).astype(bf16)
            column_z = jnp.sum(factor.astype(f32), axis=0, keepdims=True)
            total = total + dot(turned[r], ones) * column_z
        planes_ref[stop_id, rows(back), :] = jnp.concatenate(turned, axis=1)
        log_ref[stop_id] = jnp.log(total)
        for copy in keep(stop_id):
            copy.start()
        return carried

    lax.fori_loop(0, planes_ref.shape[0], of_stop, 0)


def clear(ref):
    def step(i, carried):
        ref[i] = 0
        return carried

    lax.fori_loop(0, ref.shape[0], step, 0)


def make_listing(owner_ref, tile_ref, feather_ref, weight_ref, meta_ref, codes_ref, taken_ref):
    listed = feather_ref.shape[1]
    depth = meta_ref.shape[1]
    targets = meta_ref.shape[0] // (SLOT - EDGE)
    feather = feather_ref[...].astype(f32).astype(bf16)
    key = lax.broadcasted_iota(jnp.int32, (SROWS, depth), 0)
    lane = lax.broadcasted_iota(jnp.int32, (SROWS, depth), 1)
    codes_ref[...] = turned_dot(
        feather,
        (
            ((lane < OFFSETS) & (lane % SROWS == key))
            | ((lane == EDGE_WEIGHTS) & (key == SROWS - 1))
            | ((lane == EDGE_WEIGHTS + 1) & (key == 0))
        ).astype(bf16),
    )
    lines = listed * SROWS
    line = lax.broadcasted_iota(jnp.int32, (lines, listed), 0)
    chosen = (line // SROWS == lax.broadcasted_iota(jnp.int32, (lines, listed), 1)).astype(bf16)
    own = lax.broadcasted_iota(jnp.int32, (lines, SROWS), 1) == (
        lax.broadcasted_iota(jnp.int32, (lines, SROWS), 0) % SROWS
    )
    weight_ref[...] = dot(
        jnp.where(own, dot(chosen, feather, 1), 0.0).astype(bf16), jnp.ones((SROWS, depth), bf16)
    )
    meta_ref[...] = jnp.zeros(meta_ref.shape, f32)
    at = META - EDGE
    lane = lax.broadcasted_iota(jnp.int32, (1, depth), 1)

    def add(target, row):
        meta_ref[pl.ds(target * (SLOT - EDGE) + at, 1), :] += row

    def enter(entry, carried):
        owner, tile = owner_ref[entry], tile_ref[entry]
        rank = taken_ref[owner]
        taken_ref[owner] = rank + 1
        code = codes_ref[pl.ds(entry, 1), :]
        own = (lane < OFFSETS) & (lane // SROWS == rank)
        offset = jnp.where(lane == OFFSETS + rank, tile.astype(f32), 0.0)
        add(owner, jnp.where(own, code, offset))

        @pl.when((tile == TROWS - SROWS) & (owner + 1 < targets))
        def _():
            add(owner + 1, jnp.where(lane == EDGE_WEIGHTS, code, 0.0))

        @pl.when((tile == 0) & (owner > 0))
        def _():
            add(owner - 1, jnp.where(lane == EDGE_WEIGHTS + 1, code, 0.0))

        return carried

    clear(taken_ref)
    lax.fori_loop(0, listed, enter, 0)


def rows_of(stops, lines, depth, listed, targets):
    lengths = (stops * lines, lines, listed * SROWS, targets * (SLOT - EDGE), listed, stops * SROWS)
    at = [0]
    for length in lengths:
        at.append(at[-1] + length)
    return at


def prepare_kernel(
    count,
    owner_ref,
    source_ref,
    tile_ref,
    background_ref,
    relax_ref,
    estimate_ref,
    x_ref,
    y_ref,
    z_ref,
    feather_ref,
    measured_ref,
    planes_hbm,
    rows_hbm,
    planes_ref,
    log_ref,
    block_ref,
    weight_ref,
    meta_ref,
    places_ref,
    shares_ref,
    lines_x_ref,
    lines_y_ref,
    codes_ref,
    record_ref,
    taken_ref,
    sems,
    once_sems,
):
    stops, lines, depth = log_ref.shape
    rank = z_ref.shape[1] // depth
    copy = pltpu.make_async_copy(measured_ref.at[0], record_ref, once_sems.at[0])
    copy.start()

    place = lax.axis_index("view")

    def view_of(stop_id):
        return lax.rem(lax.rem(place + stop_id, count), z_ref.shape[0])

    def keep(stop_id):
        pairs = (
            (planes_ref.at[stop_id], planes_hbm.at[stop_id]),
            (
                log_ref.at[stop_id],
                rows_hbm.at[pl.ds(pl.multiple_of(stop_id * lines, SROWS), lines)],
            ),
        )
        return [
            pltpu.make_async_copy(source, target, sems.at[k, stop_id])
            for k, (source, target) in enumerate(pairs)
        ]

    key = lax.broadcasted_iota(jnp.int32, (1, depth), 1)

    def locate(entry, carried):
        row = jnp.where(key == 0, owner_ref[entry], tile_ref[entry])
        row = jnp.where(key == 1, source_ref[entry], row)
        places_ref[pl.ds(entry, 1), :] = row.astype(f32)
        return carried

    def share(stop_id, carried):
        own = lax.broadcasted_iota(jnp.int32, background_ref.shape, 1) == view_of(stop_id)
        for k, ref in enumerate((background_ref, relax_ref)):
            value = jnp.sum(jnp.where(own, ref[...].astype(f32), 0.0), axis=1, keepdims=True)
            shares_ref[pl.ds(stop_id * SROWS + k, 1), :] = jnp.broadcast_to(value, (1, depth))
        return carried

    lax.fori_loop(0, owner_ref.shape[0], locate, 0)
    lax.fori_loop(0, stops, share, 0)
    make_planes(view_of, x_ref, y_ref, z_ref, planes_ref, log_ref, lines_x_ref, lines_y_ref, keep)
    make_listing(owner_ref, tile_ref, feather_ref, weight_ref, meta_ref, codes_ref, taken_ref)
    copy.wait()
    block_ref[...] = visit(
        estimate_ref[...],
        record_ref[...],
        planes_ref.at[0],
        log_ref.at[0],
        shares_ref[:1],
        shares_ref[1:2],
    )
    at = rows_of(stops, lines, depth, owner_ref.shape[0], meta_ref.shape[0] // (SLOT - EDGE))
    finals = [
        pltpu.make_async_copy(ref, rows_hbm.at[pl.ds(first, ref.shape[0])], once_sems.at[k])
        for k, (ref, first) in enumerate(zip((block_ref, weight_ref, meta_ref, places_ref, shares_ref), at[1:]))
    ]
    for final in finals:
        final.start()

    def settle(stop_id, carried):
        for copy in keep(stop_id):
            copy.wait()
        return carried

    lax.fori_loop(0, stops, settle, 0)
    for final in finals:
        final.wait()


def prepare(count, listing, background, relax, estimate, kernel_x, kernel_y, kernel_z, feather, measured):
    views, rank, extent_x, _ = kernel_x.shape
    extent_y = kernel_y.shape[2]
    lines, depth = estimate.shape
    stops = measured.shape[0]
    wide = rank * lines
    listed = feather.shape[1]
    factors_x = kernel_x.transpose(1, 2, 0, 3).reshape(rank * extent_x * views, extent_x)
    planes = (stops, 2 * lines + 2 * depth, wide)
    rows = max(rows_of(stops, lines, depth, listed, count)[-1], 3 * stops * planes[1])
    return pl.pallas_call(
        functools.partial(prepare_kernel, count),
        out_shape=(jax.ShapeDtypeStruct(planes, bf16), jax.ShapeDtypeStruct((rows, depth), f32)),
        in_specs=[SMEM] * 3 + [VMEM] * 7 + [ANY],
        out_specs=[ANY] * 2,
        scratch_shapes=[
            pltpu.VMEM(planes, bf16),
            pltpu.VMEM((stops, lines, depth), f32),
            pltpu.VMEM((lines, depth), f32),
            pltpu.VMEM((listed * SROWS, depth), f32),
            pltpu.VMEM((count * (SLOT - EDGE), depth), f32),
            pltpu.VMEM((listed, depth), f32),
            pltpu.VMEM((stops * SROWS, depth), f32),
            pltpu.VMEM((extent_x * views, wide), f32),
            pltpu.VMEM((views * extent_y, wide), f32),
            pltpu.VMEM((listed, depth), f32),
            pltpu.VMEM((lines, depth), bf16),
            pltpu.SMEM((count,), jnp.int32),
            pltpu.SemaphoreType.DMA((2, stops)),
            pltpu.SemaphoreType.DMA((5,)),
        ],
        compiler_params=WHOLE,
        cost_estimate=pl.CostEstimate(
            flops=views * 8 * lines * wide, bytes_accessed=views * 8 * lines * wide, transcendentals=0
        ),
    )(*listing, background, relax, estimate, factors_x, kernel_y, kernel_z, feather, measured)


def stage_kernel(start, planes_hbm, rows_hbm, planes_ref, rows_ref, log_ref, sems):
    copies = [
        pltpu.make_async_copy(source, target, sems.at[k])
        for k, (source, target) in enumerate(
            (
                (planes_hbm.at[1], planes_ref),
                (rows_hbm.at[pl.ds(start, rows_ref.shape[0])], rows_ref),
                (rows_hbm.at[pl.ds(log_ref.shape[0], log_ref.shape[0])], log_ref),
            )
        )
    ]
    for copy in copies:
        copy.start()
    for copy in copies:
        copy.wait()


def stage(planes, rows, at):
    depth = rows.shape[1]
    return pl.pallas_call(
        functools.partial(stage_kernel, at[1]),
        out_shape=(
            jax.ShapeDtypeStruct(planes.shape[1:], bf16),
            jax.ShapeDtypeStruct((at[-1] - at[1], depth), f32),
            jax.ShapeDtypeStruct((at[2] - at[1], depth), f32),
        ),
        in_specs=[ANY] * 2,
        out_specs=[VMEM] * 3,
        scratch_shapes=[pltpu.SemaphoreType.DMA((3,))],
        compiler_params=NEAR,
    )(planes, rows)


def stops_kernel(
    by_host,
    count,
    listed,
    records_ref,
    first_planes_ref,
    near_ref,
    first_log_ref,
    planes_hbm,
    rows_hbm,
    refined_hbm,
    send_ref,
    planes_ref,
    log_ref,
    block_ref,
    places_ref,
    taken_ref,
    sems,
    once_sems,
):
    stops, lines, depth = log_ref.shape
    targets = send_ref.shape[0]
    at = rows_of(stops, lines, depth, listed, targets)
    position = lax.axis_index("view")

    groups = [(2, 1)]
    while sum(groups[-1]) < stops:
        first = sum(groups[-1])
        groups.append((first, min(first - 1, stops - first)))

    def near(part):
        return near_ref[at[part] - at[1] : at[part + 1] - at[1], :]

    def log_in(stop_id):
        return pltpu.make_async_copy(
            rows_hbm.at[pl.ds(stop_id * lines, lines)], log_ref.at[stop_id], sems.at[1, stop_id]
        )

    def arrivals(group):
        first, length = groups[group]
        copies = [
            pltpu.make_async_copy(
                planes_hbm.at[pl.ds(first, length)],
                planes_ref.at[pl.ds(first, length)],
                sems.at[0, group],
            )
        ]
        return copies + [log_in(stop_id) for stop_id in range(first, first + length)]

    places_in = pltpu.make_async_copy(
        rows_hbm.at[pl.ds(at[4], listed)], places_ref, once_sems.at[0]
    )
    for group in range(len(groups)):
        for copy in arrivals(group):
            copy.start()
    places_in.start()
    clear(taken_ref)
    send_ref[:, :EDGE, :] = jnp.zeros((targets, EDGE, depth), f32)
    send_ref[:, EDGE:, :] = near(3).reshape(targets, SLOT - EDGE, depth)

    def advance(stop_id, block):
        host = lax.rem(position + stop_id, count)
        share = at[5] - at[1] + stop_id * SROWS
        return visit(
            block,
            records_ref[host if by_host else stop_id],
            first_planes_ref if stop_id == 1 else planes_ref.at[stop_id],
            first_log_ref if stop_id == 1 else log_ref.at[stop_id],
            near_ref[share : share + 1, :],
            near_ref[share + 1 : share + 2, :],
        )

    block = advance(1, near(1))
    for group, (first, length) in enumerate(groups):
        for copy in arrivals(group):
            copy.wait()
        for stop_id in range(first, first + length):
            block = advance(stop_id, block)
    block_ref[...] = block
    refined_out = pltpu.make_async_copy(block_ref, refined_hbm, once_sems.at[1])
    refined_out.start()
    places_in.wait()

    def place(entry, carried):
        owner, source, tile = (places_ref[entry, k].astype(jnp.int32) for k in range(3))
        rank = taken_ref[owner]
        taken_ref[owner] = rank + 1
        weights = near_ref[pl.ds(pl.multiple_of(at[2] - at[1] + entry * SROWS, SROWS), SROWS), :]
        piece = block_ref[pl.ds(source, SROWS), :] * weights
        send_ref[owner, pl.ds(pl.multiple_of(rank * SROWS, SROWS), SROWS), :] = piece

        @pl.when((tile == TROWS - SROWS) & (owner + 1 < targets))
        def _():
            send_ref[owner + 1, EDGE : EDGE + 1, :] += piece[SROWS - 1 :]

        @pl.when((tile == 0) & (owner > 0))
        def _():
            send_ref[owner - 1, EDGE + 1 : EDGE + 2, :] += piece[:1]

        return carried

    lax.fori_loop(0, listed, place, 0)
    refined_out.wait()


def run_stops(by_host, count, listed, records, planes, rows):
    stops, lines, depth = records.shape
    first_planes, near, first_log = stage(planes, rows, rows_of(stops, lines, depth, listed, count))
    return pl.pallas_call(
        functools.partial(stops_kernel, by_host, count, listed),
        out_shape=(
            jax.ShapeDtypeStruct((lines, depth), f32),
            jax.ShapeDtypeStruct((count, SLOT, depth), f32),
        ),
        in_specs=[VMEM] * 4 + [ANY] * 2,
        out_specs=(ANY, VMEM),
        scratch_shapes=[
            pltpu.VMEM(planes.shape, planes.dtype),
            pltpu.VMEM((stops, lines, depth), f32),
            pltpu.VMEM((lines, depth), f32),
            pltpu.SMEM((listed, depth), f32),
            pltpu.SMEM((count,), jnp.int32),
            pltpu.SemaphoreType.DMA((2, stops)),
            pltpu.SemaphoreType.DMA((2,)),
        ],
        compiler_params=NEAR,
    )(records, first_planes, near, first_log, planes, rows)


def blend_kernel(data_ref, smoothed_ref):
    count, _, depth = data_ref.shape
    place = lax.axis_index("view")
    slots = count * EDGE
    meta = data_ref[:, META, :]
    key = lax.broadcasted_iota(jnp.int32, (depth, slots), 0)
    column = lax.broadcasted_iota(jnp.int32, (depth, slots), 1) % EDGE
    spread_weight = (key == column).astype(bf16)
    spread_offset = (key == OFFSETS + column // SROWS).astype(bf16)
    own = lax.broadcasted_iota(jnp.int32, (count, slots), 0) == (
        lax.broadcasted_iota(jnp.int32, (count, slots), 1) // EDGE
    )
    coded = meta.astype(bf16)
    weight = jnp.sum(jnp.where(own, dot(coded, spread_weight), 0.0), axis=0, keepdims=True)
    offset = jnp.sum(jnp.where(own, dot(coded, spread_offset), 0.0), axis=0, keepdims=True)
    line = offset.astype(jnp.int32) + lax.broadcasted_iota(jnp.int32, (1, slots), 1) % SROWS
    placed = (line == lax.broadcasted_iota(jnp.int32, (TROWS, slots), 0)).astype(f32)
    data = data_ref[:, :EDGE, :].reshape(slots, depth)
    numerator = 1.0 + jnp.dot(
        placed, data, preferred_element_type=f32, precision=lax.Precision.HIGHEST
    )
    denominator = 1.0 + jnp.sum(placed * weight, axis=1, keepdims=True)
    joined = numerator / denominator

    def edge(which, inside):
        top = 1.0 + jnp.sum(data_ref[:, EDGE + which, :], axis=0, keepdims=True)
        lane = EDGE_WEIGHTS + which
        below = 1.0 + jnp.sum(meta[:, lane : lane + 1], axis=0, keepdims=True)
        return jnp.where(inside, top / below, 0.0)

    behind = edge(0, place > 0)
    beyond = edge(1, place < count - 1)
    side = jnp.zeros((TROWS, 1), f32)
    flux = jnp.zeros_like(joined)
    for neighbor in (
        jnp.concatenate([joined[1:], beyond], axis=0),
        jnp.concatenate([behind, joined[:-1]], axis=0),
        jnp.concatenate([joined[:, 1:], side], axis=1),
        jnp.concatenate([side, joined[:, :-1]], axis=1),
    ):
        change = neighbor - joined
        flux = flux + change / (1.0 + change / edge_scale * (change / edge_scale))
    smoothed_ref[...] = joined + smooth_rate * flux


def blend(data):
    return pl.pallas_call(
        blend_kernel,
        out_shape=jax.ShapeDtypeStruct((TROWS, data.shape[2]), f32),
        in_specs=[VMEM],
        out_specs=VMEM,
        compiler_params=pltpu.CompilerParams(vmem_limit_bytes=32 << 20),
    )(data)


def on_device(
    estimate,
    measured,
    kernel_z,
    kernel_x,
    kernel_y,
    background,
    relax,
    owner,
    source_offset,
    tile_offset,
    feather,
):
    count = lax.axis_size("view")
    stops = measured.shape[0]
    views, rank, depth, _ = kernel_z.shape
    by_host = stops == count
    if by_host:
        records = lax.all_to_all(
            by_target(measured), "view", split_axis=0, concat_axis=0, tiled=True
        )
    else:
        arrived = [measured[0]]
        for stop_id in range(1, stops):
            route = [((i + stop_id) % count, i) for i in range(count)]
            arrived.append(lax.ppermute(measured[stop_id], "view", route))
        records = jnp.stack(arrived, axis=0)

    factors_z = kernel_z.reshape(views, rank * depth, depth)
    planes, rows = prepare(
        count,
        (owner[:, 0], source_offset, tile_offset),
        background[None],
        relax[None],
        estimate,
        kernel_x,
        kernel_y,
        factors_z,
        feather.T,
        measured,
    )
    refined, outgoing = run_stops(by_host, count, feather.shape[0], records, planes, rows)
    incoming = lax.all_to_all(outgoing, "view", split_axis=0, concat_axis=0, tiled=True)
    return refined, blend(incoming)


def solution(mesh):
    lined = P(("groups", "view"))
    return jax.shard_map(
        on_device,
        mesh=mesh,
        in_specs=(
            P(("groups", "view"), None),
            P(("groups", "view"), None, None),
            P(),
            P(),
            P(),
            P(),
            P(),
            P(("groups", "view"), None),
            lined,
            lined,
            P(("groups", "view"), None),
        ),
        out_specs=(P(("groups", "view"), None), P(("groups", "view"), None)),
        check_vma=False,
    )
```

```python
import functools

import jax
import jax.numpy as jnp
from jax import lax
from jax.experimental import pallas as pl
from jax.experimental.pallas import tpu as pltpu
from jax.sharding import PartitionSpec as P

SROWS = 8
TROWS = 64
CAP = 2
EDGE = CAP * SROWS
META = EDGE + 2
SLOT = 24
OFFSETS = CAP * SROWS
EDGE_WEIGHTS = OFFSETS + CAP

smooth_rate = 0.24
edge_scale = 1.0

f32 = jnp.float32
bf16 = jnp.bfloat16
VMEM = pl.BlockSpec(memory_space=pltpu.VMEM)
SMEM = pl.BlockSpec(memory_space=pltpu.SMEM)
ANY = pl.BlockSpec(memory_space=pl.ANY)
NEAR = pltpu.CompilerParams(vmem_limit_bytes=51 << 20)
WHOLE = pltpu.CompilerParams(vmem_limit_bytes=60 << 20)


def dot(a, b, axis=0):
    return lax.dot_general(a, b, (((1,), (axis,)), ((), ())), preferred_element_type=f32)


def turned_dot(a, b):
    return lax.dot_general(a, b, (((0,), (0,)), ((), ())), preferred_element_type=f32)


def plane_rows(lines, depth):
    toward = (0, depth)
    front = (depth, lines)
    back_z = (depth + lines, depth)
    back = (2 * depth + lines, lines)
    return toward, front, back_z, back


def visit(block, record, planes_ref, log_ref, back_value, relax_value, ready=None):
    lines, depth = block.shape
    rank = planes_ref.shape[1] // lines

    def part(which):
        if ready is not None:
            ready(which)
        first, length = plane_rows(lines, depth)[which]
        return planes_ref[first : first + length, :]

    def along(rows, which):
        factors = part(which)
        parts = [dot(rows, factors[:, r * depth : (r + 1) * depth]).astype(bf16) for r in range(rank)]
        return jnp.concatenate(parts, axis=0)

    def across(which, stacked):
        plane = part(which)
        cut = 2 * depth
        return dot(plane[:, :cut], stacked[:cut]) + dot(plane[:, cut:], stacked[cut:])

    along_z = along(block.astype(bf16), 0)
    forward = across(1, along_z)
    ratio = (record.astype(f32) / (forward + back_value)).astype(bf16)
    back_z = along(ratio, 2)
    adjoint = across(3, back_z)
    if ready is not None:
        ready(4)
    return block * jnp.exp(relax_value * (jnp.log(adjoint) - log_ref[...]))


def by_target_kernel(source_ref, target_ref, held_ref, in_sems, out_sems):
    count = target_ref.shape[0]
    place = lax.axis_index("view")
    arrivals, departures = [], []
    for target in range(count):
        stop_id = lax.rem(place + count - target, count)
        arrivals.append(
            pltpu.make_async_copy(source_ref.at[stop_id], held_ref.at[target], in_sems.at[target])
        )
        departures.append(
            pltpu.make_async_copy(held_ref.at[target], target_ref.at[target], out_sems.at[target])
        )
    for arrival in arrivals:
        arrival.start()
    for arrival, departure in zip(arrivals, departures):
        arrival.wait()
        departure.start()
    for departure in departures:
        departure.wait()


def by_target(measured):
    count = measured.shape[0]
    return pl.pallas_call(
        by_target_kernel,
        out_shape=jax.ShapeDtypeStruct(measured.shape, measured.dtype),
        in_specs=[ANY],
        out_specs=ANY,
        scratch_shapes=[
            pltpu.VMEM(measured.shape, measured.dtype),
            pltpu.SemaphoreType.DMA((count,)),
            pltpu.SemaphoreType.DMA((count,)),
        ],
        compiler_params=WHOLE,
    )(measured)


def make_planes(view_of, x_ref, y_ref, z_ref, planes_ref, log_ref, lines_x_ref, lines_y_ref, keep):
    views, rank, extent_y, _ = y_ref.shape
    extent_x = x_ref.shape[1]
    depth = z_ref.shape[2]
    lines = extent_x * extent_y
    wide = rank * lines

    def spread(extent, of_x, r):
        row = lax.broadcasted_iota(jnp.int32, (extent, wide), 0)
        column = lax.broadcasted_iota(jnp.int32, (extent, wide), 1) - r * lines
        inside = (column >= 0) & (column < lines)
        return (inside & (row == (column // extent_y if of_x else column % extent_y))).astype(bf16)

    held = extent_x * views
    lines_x_ref[...] = sum(
        dot(x_ref[r * held : (r + 1) * held, :], spread(extent_x, True, r)) for r in range(rank)
    )
    lines_y_ref[...] = sum(
        dot(y_ref[:, r].reshape(views * extent_y, extent_y), spread(extent_y, False, r))
        for r in range(rank)
    )
    ones = jnp.ones((lines, depth), bf16)

    def diagonal(extent):
        row = lax.broadcasted_iota(jnp.int32, (extent, extent), 0)
        return (row == lax.broadcasted_iota(jnp.int32, (extent, extent), 1)).astype(bf16)

    toward, front, back_z, back = plane_rows(lines, depth)

    def rows(part):
        return slice(part[0], part[0] + part[1])

    def of_stop(stop_id, carried):
        view_id = view_of(stop_id)
        first = pl.multiple_of(view_id * extent_y, extent_y)
        lines_y = lines_y_ref[pl.ds(first, extent_y), :]
        for x in range(extent_x):
            line_x = lines_x_ref[pl.ds(x * views + view_id, 1), :]
            at = front[0] + x * extent_y
            planes_ref[stop_id, at : at + extent_y, :] = (line_x * lines_y).astype(bf16)
        total = jnp.zeros((lines, depth), f32)
        turned = []
        for r in range(rank):
            plane = planes_ref[stop_id, rows(front), r * lines : (r + 1) * lines]
            turned.append(dot(diagonal(lines), plane, 1).astype(bf16))
            factor = z_ref[view_id, r * depth : (r + 1) * depth, :]
            columns = slice(r * depth, (r + 1) * depth)
            planes_ref[stop_id, rows(back_z), columns] = factor
            planes_ref[stop_id, rows(toward), columns] = dot(diagonal(depth), factor, 1).astype(bf16)
            column_z = jnp.sum(factor.astype(f32), axis=0, keepdims=True)
            total = total + dot(turned[r], ones) * column_z
        planes_ref[stop_id, rows(back), :] = jnp.concatenate(turned, axis=1)
        log_ref[stop_id] = jnp.log(total)
        for copy in keep(stop_id):
            copy.start()
        return carried

    lax.fori_loop(0, planes_ref.shape[0], of_stop, 0)


def clear(ref):
    def step(i, carried):
        ref[i] = 0
        return carried

    lax.fori_loop(0, ref.shape[0], step, 0)


def make_listing(owner_ref, tile_ref, feather_ref, weight_ref, meta_ref, codes_ref, taken_ref):
    listed = feather_ref.shape[1]
    depth = meta_ref.shape[1]
    targets = meta_ref.shape[0] // (SLOT - EDGE)
    feather = feather_ref[...].astype(f32).astype(bf16)
    key = lax.broadcasted_iota(jnp.int32, (SROWS, depth), 0)
    lane = lax.broadcasted_iota(jnp.int32, (SROWS, depth), 1)
    codes_ref[...] = turned_dot(
        feather,
        (
            ((lane < OFFSETS) & (lane % SROWS == key))
            | ((lane == EDGE_WEIGHTS) & (key == SROWS - 1))
            | ((lane == EDGE_WEIGHTS + 1) & (key == 0))
        ).astype(bf16),
    )
    lines = listed * SROWS
    line = lax.broadcasted_iota(jnp.int32, (lines, listed), 0)
    chosen = (line // SROWS == lax.broadcasted_iota(jnp.int32, (lines, listed), 1)).astype(bf16)
    own = lax.broadcasted_iota(jnp.int32, (lines, SROWS), 1) == (
        lax.broadcasted_iota(jnp.int32, (lines, SROWS), 0) % SROWS
    )
    weight_ref[...] = dot(
        jnp.where(own, dot(chosen, feather, 1), 0.0).astype(bf16), jnp.ones((SROWS, depth), bf16)
    )
    meta_ref[...] = jnp.zeros(meta_ref.shape, f32)
    at = META - EDGE
    lane = lax.broadcasted_iota(jnp.int32, (1, depth), 1)

    def add(target, row):
        meta_ref[pl.ds(target * (SLOT - EDGE) + at, 1), :] += row

    def enter(entry, carried):
        owner, tile = owner_ref[entry], tile_ref[entry]
        rank = taken_ref[owner]
        taken_ref[owner] = rank + 1
        code = codes_ref[pl.ds(entry, 1), :]
        own = (lane < OFFSETS) & (lane // SROWS == rank)
        offset = jnp.where(lane == OFFSETS + rank, tile.astype(f32), 0.0)
        add(owner, jnp.where(own, code, offset))

        @pl.when((tile == TROWS - SROWS) & (owner + 1 < targets))
        def _():
            add(owner + 1, jnp.where(lane == EDGE_WEIGHTS, code, 0.0))

        @pl.when((tile == 0) & (owner > 0))
        def _():
            add(owner - 1, jnp.where(lane == EDGE_WEIGHTS + 1, code, 0.0))

        return carried

    clear(taken_ref)
    lax.fori_loop(0, listed, enter, 0)


def rows_of(stops, lines, depth, listed, targets):
    lengths = (stops * lines, lines, listed * SROWS, targets * (SLOT - EDGE), listed, stops * SROWS)
    at = [0]
    for length in lengths:
        at.append(at[-1] + length)
    return at


def prepare_kernel(
    count,
    owner_ref,
    source_ref,
    tile_ref,
    background_ref,
    relax_ref,
    estimate_ref,
    x_ref,
    y_ref,
    z_ref,
    feather_ref,
    measured_ref,
    planes_hbm,
    rows_hbm,
    planes_ref,
    log_ref,
    block_ref,
    weight_ref,
    meta_ref,
    places_ref,
    shares_ref,
    lines_x_ref,
    lines_y_ref,
    codes_ref,
    record_ref,
    taken_ref,
    sems,
    once_sems,
):
    stops, lines, depth = log_ref.shape
    rank = z_ref.shape[1] // depth
    copy = pltpu.make_async_copy(measured_ref.at[0], record_ref, once_sems.at[0])
    copy.start()

    place = lax.axis_index("view")

    def view_of(stop_id):
        return lax.rem(lax.rem(place + stop_id, count), z_ref.shape[0])

    def keep(stop_id):
        pairs = (
            (planes_ref.at[stop_id], planes_hbm.at[stop_id]),
            (
                log_ref.at[stop_id],
                rows_hbm.at[pl.ds(pl.multiple_of(stop_id * lines, SROWS), lines)],
            ),
        )
        return [
            pltpu.make_async_copy(source, target, sems.at[k, stop_id])
            for k, (source, target) in enumerate(pairs)
        ]

    key = lax.broadcasted_iota(jnp.int32, (1, depth), 1)

    def locate(entry, carried):
        row = jnp.where(key == 0, owner_ref[entry], tile_ref[entry])
        row = jnp.where(key == 1, source_ref[entry], row)
        places_ref[pl.ds(entry, 1), :] = row.astype(f32)
        return carried

    def share(stop_id, carried):
        own = lax.broadcasted_iota(jnp.int32, background_ref.shape, 1) == view_of(stop_id)
        for k, ref in enumerate((background_ref, relax_ref)):
            value = jnp.sum(jnp.where(own, ref[...].astype(f32), 0.0), axis=1, keepdims=True)
            shares_ref[pl.ds(stop_id * SROWS + k, 1), :] = jnp.broadcast_to(value, (1, depth))
        return carried

    lax.fori_loop(0, owner_ref.shape[0], locate, 0)
    lax.fori_loop(0, stops, share, 0)
    make_planes(view_of, x_ref, y_ref, z_ref, planes_ref, log_ref, lines_x_ref, lines_y_ref, keep)
    make_listing(owner_ref, tile_ref, feather_ref, weight_ref, meta_ref, codes_ref, taken_ref)
    copy.wait()
    block_ref[...] = visit(
        estimate_ref[...],
        record_ref[...],
        planes_ref.at[0],
        log_ref.at[0],
        shares_ref[:1],
        shares_ref[1:2],
    )
    at = rows_of(stops, lines, depth, owner_ref.shape[0], meta_ref.shape[0] // (SLOT - EDGE))
    finals = [
        pltpu.make_async_copy(ref, rows_hbm.at[pl.ds(first, ref.shape[0])], once_sems.at[k])
        for k, (ref, first) in enumerate(zip((block_ref, weight_ref, meta_ref, places_ref, shares_ref), at[1:]))
    ]
    for final in finals:
        final.start()

    def settle(stop_id, carried):
        for copy in keep(stop_id):
            copy.wait()
        return carried

    lax.fori_loop(0, stops, settle, 0)
    for final in finals:
        final.wait()


def prepare(count, listing, background, relax, estimate, kernel_x, kernel_y, kernel_z, feather, measured):
    views, rank, extent_x, _ = kernel_x.shape
    extent_y = kernel_y.shape[2]
    lines, depth = estimate.shape
    stops = measured.shape[0]
    wide = rank * lines
    listed = feather.shape[1]
    factors_x = kernel_x.transpose(1, 2, 0, 3).reshape(rank * extent_x * views, extent_x)
    planes = (stops, 2 * lines + 2 * depth, wide)
    rows = max(rows_of(stops, lines, depth, listed, count)[-1], 3 * stops * planes[1])
    return pl.pallas_call(
        functools.partial(prepare_kernel, count),
        out_shape=(jax.ShapeDtypeStruct(planes, bf16), jax.ShapeDtypeStruct((rows, depth), f32)),
        in_specs=[SMEM] * 3 + [VMEM] * 7 + [ANY],
        out_specs=[ANY] * 2,
        scratch_shapes=[
            pltpu.VMEM(planes, bf16),
            pltpu.VMEM((stops, lines, depth), f32),
            pltpu.VMEM((lines, depth), f32),
            pltpu.VMEM((listed * SROWS, depth), f32),
            pltpu.VMEM((count * (SLOT - EDGE), depth), f32),
            pltpu.VMEM((listed, depth), f32),
            pltpu.VMEM((stops * SROWS, depth), f32),
            pltpu.VMEM((extent_x * views, wide), f32),
            pltpu.VMEM((views * extent_y, wide), f32),
            pltpu.VMEM((listed, depth), f32),
            pltpu.VMEM((lines, depth), bf16),
            pltpu.SMEM((count,), jnp.int32),
            pltpu.SemaphoreType.DMA((2, stops)),
            pltpu.SemaphoreType.DMA((5,)),
        ],
        compiler_params=WHOLE,
        cost_estimate=pl.CostEstimate(
            flops=views * 8 * lines * wide, bytes_accessed=views * 8 * lines * wide, transcendentals=0
        ),
    )(*listing, background, relax, estimate, factors_x, kernel_y, kernel_z, feather, measured)


def stage_kernel(start, planes_hbm, rows_hbm, planes_ref, rows_ref, log_ref, sems):
    copies = [
        pltpu.make_async_copy(source, target, sems.at[k])
        for k, (source, target) in enumerate(
            (
                (planes_hbm.at[1], planes_ref),
                (rows_hbm.at[pl.ds(start, rows_ref.shape[0])], rows_ref),
                (rows_hbm.at[pl.ds(log_ref.shape[0], log_ref.shape[0])], log_ref),
            )
        )
    ]
    for copy in copies:
        copy.start()
    for copy in copies:
        copy.wait()


def stage(planes, rows, at):
    depth = rows.shape[1]
    return pl.pallas_call(
        functools.partial(stage_kernel, at[1]),
        out_shape=(
            jax.ShapeDtypeStruct(planes.shape[1:], bf16),
            jax.ShapeDtypeStruct((at[-1] - at[1], depth), f32),
            jax.ShapeDtypeStruct((at[2] - at[1], depth), f32),
        ),
        in_specs=[ANY] * 2,
        out_specs=[VMEM] * 3,
        scratch_shapes=[pltpu.SemaphoreType.DMA((3,))],
        compiler_params=NEAR,
    )(planes, rows)


def stops_kernel(
    by_host,
    count,
    listed,
    records_ref,
    first_planes_ref,
    near_ref,
    first_log_ref,
    planes_hbm,
    rows_hbm,
    refined_hbm,
    send_ref,
    planes_ref,
    log_ref,
    block_ref,
    places_ref,
    taken_ref,
    sems,
    once_sems,
):
    stops, lines, depth = log_ref.shape
    targets = send_ref.shape[0]
    at = rows_of(stops, lines, depth, listed, targets)
    position = lax.axis_index("view")

    groups = [(2, 1)]
    while sum(groups[-1]) < stops:
        first = sum(groups[-1])
        groups.append((first, min(len(groups) + 1, stops - first)))

    def near(part):
        return near_ref[at[part] - at[1] : at[part + 1] - at[1], :]

    def log_in(stop_id):
        return pltpu.make_async_copy(
            rows_hbm.at[pl.ds(stop_id * lines, lines)], log_ref.at[stop_id], sems.at[1, stop_id]
        )

    def arrivals(group):
        first, length = groups[group]
        copies = [
            pltpu.make_async_copy(
                planes_hbm.at[pl.ds(first, length)],
                planes_ref.at[pl.ds(first, length)],
                sems.at[0, group],
            )
        ]
        return copies + [log_in(stop_id) for stop_id in range(first, first + length)]

    places_in = pltpu.make_async_copy(
        rows_hbm.at[pl.ds(at[4], listed)], places_ref, once_sems.at[0]
    )
    for group in range(len(groups)):
        for copy in arrivals(group):
            copy.start()
    places_in.start()
    clear(taken_ref)
    send_ref[:, :EDGE, :] = jnp.zeros((targets, EDGE, depth), f32)
    send_ref[:, EDGE:, :] = near(3).reshape(targets, SLOT - EDGE, depth)

    def advance(stop_id, block):
        host = lax.rem(position + stop_id, count)
        share = at[5] - at[1] + stop_id * SROWS
        return visit(
            block,
            records_ref[host if by_host else stop_id],
            first_planes_ref if stop_id == 1 else planes_ref.at[stop_id],
            first_log_ref if stop_id == 1 else log_ref.at[stop_id],
            near_ref[share : share + 1, :],
            near_ref[share + 1 : share + 2, :],
        )

    block = advance(1, near(1))
    for group, (first, length) in enumerate(groups):
        for copy in arrivals(group):
            copy.wait()
        for stop_id in range(first, first + length):
            block = advance(stop_id, block)
    block_ref[...] = block
    refined_out = pltpu.make_async_copy(block_ref, refined_hbm, once_sems.at[1])
    refined_out.start()
    places_in.wait()

    def place(entry, carried):
        owner, source, tile = (places_ref[entry, k].astype(jnp.int32) for k in range(3))
        rank = taken_ref[owner]
        taken_ref[owner] = rank + 1
        weights = near_ref[pl.ds(pl.multiple_of(at[2] - at[1] + entry * SROWS, SROWS), SROWS), :]
        piece = block_ref[pl.ds(source, SROWS), :] * weights
        send_ref[owner, pl.ds(pl.multiple_of(rank * SROWS, SROWS), SROWS), :] = piece

        @pl.when((tile == TROWS - SROWS) & (owner + 1 < targets))
        def _():
            send_ref[owner + 1, EDGE : EDGE + 1, :] += piece[SROWS - 1 :]

        @pl.when((tile == 0) & (owner > 0))
        def _():
            send_ref[owner - 1, EDGE + 1 : EDGE + 2, :] += piece[:1]

        return carried

    lax.fori_loop(0, listed, place, 0)
    refined_out.wait()


def run_stops(by_host, count, listed, records, planes, rows):
    stops, lines, depth = records.shape
    first_planes, near, first_log = stage(planes, rows, rows_of(stops, lines, depth, listed, count))
    return pl.pallas_call(
        functools.partial(stops_kernel, by_host, count, listed),
        out_shape=(
            jax.ShapeDtypeStruct((lines, depth), f32),
            jax.ShapeDtypeStruct((count, SLOT, depth), f32),
        ),
        in_specs=[VMEM] * 4 + [ANY] * 2,
        out_specs=(ANY, VMEM),
        scratch_shapes=[
            pltpu.VMEM(planes.shape, planes.dtype),
            pltpu.VMEM((stops, lines, depth), f32),
            pltpu.VMEM((lines, depth), f32),
            pltpu.SMEM((listed, depth), f32),
            pltpu.SMEM((count,), jnp.int32),
            pltpu.SemaphoreType.DMA((2, stops)),
            pltpu.SemaphoreType.DMA((2,)),
        ],
        compiler_params=NEAR,
    )(records, first_planes, near, first_log, planes, rows)


def blend_kernel(data_ref, smoothed_ref):
    count, _, depth = data_ref.shape
    place = lax.axis_index("view")
    slots = count * EDGE
    meta = data_ref[:, META, :]
    key = lax.broadcasted_iota(jnp.int32, (depth, slots), 0)
    column = lax.broadcasted_iota(jnp.int32, (depth, slots), 1) % EDGE
    spread_weight = (key == column).astype(bf16)
    spread_offset = (key == OFFSETS + column // SROWS).astype(bf16)
    own = lax.broadcasted_iota(jnp.int32, (count, slots), 0) == (
        lax.broadcasted_iota(jnp.int32, (count, slots), 1) // EDGE
    )
    coded = meta.astype(bf16)
    weight = jnp.sum(jnp.where(own, dot(coded, spread_weight), 0.0), axis=0, keepdims=True)
    offset = jnp.sum(jnp.where(own, dot(coded, spread_offset), 0.0), axis=0, keepdims=True)
    line = offset.astype(jnp.int32) + lax.broadcasted_iota(jnp.int32, (1, slots), 1) % SROWS
    placed = (line == lax.broadcasted_iota(jnp.int32, (TROWS, slots), 0)).astype(f32)
    data = data_ref[:, :EDGE, :].reshape(slots, depth)
    numerator = 1.0 + jnp.dot(
        placed, data, preferred_element_type=f32, precision=lax.Precision.HIGHEST
    )
    denominator = 1.0 + jnp.sum(placed * weight, axis=1, keepdims=True)
    joined = numerator / denominator

    def edge(which, inside):
        top = 1.0 + jnp.sum(data_ref[:, EDGE + which, :], axis=0, keepdims=True)
        lane = EDGE_WEIGHTS + which
        below = 1.0 + jnp.sum(meta[:, lane : lane + 1], axis=0, keepdims=True)
        return jnp.where(inside, top / below, 0.0)

    behind = edge(0, place > 0)
    beyond = edge(1, place < count - 1)
    side = jnp.zeros((TROWS, 1), f32)
    flux = jnp.zeros_like(joined)
    for neighbor in (
        jnp.concatenate([joined[1:], beyond], axis=0),
        jnp.concatenate([behind, joined[:-1]], axis=0),
        jnp.concatenate([joined[:, 1:], side], axis=1),
        jnp.concatenate([side, joined[:, :-1]], axis=1),
    ):
        change = neighbor - joined
        flux = flux + change / (1.0 + change / edge_scale * (change / edge_scale))
    smoothed_ref[...] = joined + smooth_rate * flux


def blend(data):
    return pl.pallas_call(
        blend_kernel,
        out_shape=jax.ShapeDtypeStruct((TROWS, data.shape[2]), f32),
        in_specs=[VMEM],
        out_specs=VMEM,
        compiler_params=pltpu.CompilerParams(vmem_limit_bytes=32 << 20),
    )(data)


def on_device(
    estimate,
    measured,
    kernel_z,
    kernel_x,
    kernel_y,
    background,
    relax,
    owner,
    source_offset,
    tile_offset,
    feather,
):
    count = lax.axis_size("view")
    stops = measured.shape[0]
    views, rank, depth, _ = kernel_z.shape
    by_host = stops == count
    if by_host:
        records = lax.all_to_all(
            by_target(measured), "view", split_axis=0, concat_axis=0, tiled=True
        )
    else:
        arrived = [measured[0]]
        for stop_id in range(1, stops):
            route = [((i + stop_id) % count, i) for i in range(count)]
            arrived.append(lax.ppermute(measured[stop_id], "view", route))
        records = jnp.stack(arrived, axis=0)

    factors_z = kernel_z.reshape(views, rank * depth, depth)
    planes, rows = prepare(
        count,
        (owner[:, 0], source_offset, tile_offset),
        background[None],
        relax[None],
        estimate,
        kernel_x,
        kernel_y,
        factors_z,
        feather.T,
        measured,
    )
    refined, outgoing = run_stops(by_host, count, feather.shape[0], records, planes, rows)
    incoming = lax.all_to_all(outgoing, "view", split_axis=0, concat_axis=0, tiled=True)
    return refined, blend(incoming)


def solution(mesh):
    lined = P(("groups", "view"))
    return jax.shard_map(
        on_device,
        mesh=mesh,
        in_specs=(
            P(("groups", "view"), None),
            P(("groups", "view"), None, None),
            P(),
            P(),
            P(),
            P(),
            P(),
            P(("groups", "view"), None),
            lined,
            lined,
            P(("groups", "view"), None),
        ),
        out_specs=(P(("groups", "view"), None), P(("groups", "view"), None)),
        check_vma=False,
    )
```

```python
import functools

import jax
import jax.numpy as jnp
from jax import lax
from jax.experimental import pallas as pl
from jax.experimental.pallas import tpu as pltpu
from jax.sharding import PartitionSpec as P

SROWS = 8
TROWS = 64
CAP = 2
EDGE = CAP * SROWS
META = EDGE + 2
SLOT = 24
OFFSETS = CAP * SROWS
EDGE_WEIGHTS = OFFSETS + CAP

smooth_rate = 0.24
edge_scale = 1.0

f32 = jnp.float32
bf16 = jnp.bfloat16
VMEM = pl.BlockSpec(memory_space=pltpu.VMEM)
SMEM = pl.BlockSpec(memory_space=pltpu.SMEM)
ANY = pl.BlockSpec(memory_space=pl.ANY)
NEAR = pltpu.CompilerParams(vmem_limit_bytes=51 << 20)
WHOLE = pltpu.CompilerParams(vmem_limit_bytes=60 << 20)


def dot(a, b, axis=0):
    return lax.dot_general(a, b, (((1,), (axis,)), ((), ())), preferred_element_type=f32)


def turned_dot(a, b):
    return lax.dot_general(a, b, (((0,), (0,)), ((), ())), preferred_element_type=f32)


def plane_rows(lines, depth):
    toward = (0, depth)
    front = (depth, lines)
    back_z = (depth + lines, depth)
    back = (2 * depth + lines, lines)
    return toward, front, back_z, back


def visit(block, record, planes_ref, log_ref, back_value, relax_value, ready=None):
    lines, depth = block.shape
    rank = planes_ref.shape[1] // lines

    def part(which):
        if ready is not None:
            ready(which)
        first, length = plane_rows(lines, depth)[which]
        return planes_ref[first : first + length, :]

    def along(rows, which):
        factors = part(which)
        parts = [dot(rows, factors[:, r * depth : (r + 1) * depth]).astype(bf16) for r in range(rank)]
        return jnp.concatenate(parts, axis=0)

    def across(which, stacked):
        plane = part(which)
        cut = 2 * depth
        return dot(plane[:, :cut], stacked[:cut]) + dot(plane[:, cut:], stacked[cut:])

    along_z = along(block.astype(bf16), 0)
    forward = across(1, along_z)
    ratio = (record.astype(f32) / (forward + back_value)).astype(bf16)
    back_z = along(ratio, 2)
    adjoint = across(3, back_z)
    if ready is not None:
        ready(4)
    return block * jnp.exp(relax_value * (jnp.log(adjoint) - log_ref[...]))


def by_target_kernel(source_ref, target_ref, held_ref, in_sems, out_sems):
    count = target_ref.shape[0]
    place = lax.axis_index("view")
    arrivals, departures = [], []
    for target in range(count):
        stop_id = lax.rem(place + count - target, count)
        arrivals.append(
            pltpu.make_async_copy(source_ref.at[stop_id], held_ref.at[target], in_sems.at[target])
        )
        departures.append(
            pltpu.make_async_copy(held_ref.at[target], target_ref.at[target], out_sems.at[target])
        )
    for arrival in arrivals:
        arrival.start()
    for arrival, departure in zip(arrivals, departures):
        arrival.wait()
        departure.start()
    for departure in departures:
        departure.wait()


def by_target(measured):
    count = measured.shape[0]
    return pl.pallas_call(
        by_target_kernel,
        out_shape=jax.ShapeDtypeStruct(measured.shape, measured.dtype),
        in_specs=[ANY],
        out_specs=ANY,
        scratch_shapes=[
            pltpu.VMEM(measured.shape, measured.dtype),
            pltpu.SemaphoreType.DMA((count,)),
            pltpu.SemaphoreType.DMA((count,)),
        ],
        compiler_params=WHOLE,
    )(measured)


def make_planes(view_of, x_ref, y_ref, z_ref, planes_ref, log_ref, lines_x_ref, lines_y_ref, keep):
    views, rank, extent_y, _ = y_ref.shape
    extent_x = x_ref.shape[1]
    depth = z_ref.shape[2]
    lines = extent_x * extent_y
    wide = rank * lines

    def spread(extent, of_x, r):
        row = lax.broadcasted_iota(jnp.int32, (extent, wide), 0)
        column = lax.broadcasted_iota(jnp.int32, (extent, wide), 1) - r * lines
        inside = (column >= 0) & (column < lines)
        return (inside & (row == (column // extent_y if of_x else column % extent_y))).astype(bf16)

    held = extent_x * views
    lines_x_ref[...] = sum(
        dot(x_ref[r * held : (r + 1) * held, :], spread(extent_x, True, r)) for r in range(rank)
    )
    lines_y_ref[...] = sum(
        dot(y_ref[:, r].reshape(views * extent_y, extent_y), spread(extent_y, False, r))
        for r in range(rank)
    )
    ones = jnp.ones((lines, depth), bf16)

    def diagonal(extent):
        row = lax.broadcasted_iota(jnp.int32, (extent, extent), 0)
        return (row == lax.broadcasted_iota(jnp.int32, (extent, extent), 1)).astype(bf16)

    toward, front, back_z, back = plane_rows(lines, depth)

    def rows(part):
        return slice(part[0], part[0] + part[1])

    def of_stop(stop_id, carried):
        view_id = view_of(stop_id)
        first = pl.multiple_of(view_id * extent_y, extent_y)
        lines_y = lines_y_ref[pl.ds(first, extent_y), :]
        for x in range(extent_x):
            line_x = lines_x_ref[pl.ds(x * views + view_id, 1), :]
            at = front[0] + x * extent_y
            planes_ref[stop_id, at : at + extent_y, :] = (line_x * lines_y).astype(bf16)
        total = jnp.zeros((lines, depth), f32)
        turned = []
        for r in range(rank):
            plane = planes_ref[stop_id, rows(front), r * lines : (r + 1) * lines]
            turned.append(dot(diagonal(lines), plane, 1).astype(bf16))
            factor = z_ref[view_id, r * depth : (r + 1) * depth, :]
            columns = slice(r * depth, (r + 1) * depth)
            planes_ref[stop_id, rows(back_z), columns] = factor
            planes_ref[stop_id, rows(toward), columns] = dot(diagonal(depth), factor, 1).astype(bf16)
            column_z = jnp.sum(factor.astype(f32), axis=0, keepdims=True)
            total = total + dot(turned[r], ones) * column_z
        planes_ref[stop_id, rows(back), :] = jnp.concatenate(turned, axis=1)
        log_ref[stop_id] = jnp.log(total)
        for copy in keep(stop_id):
            copy.start()
        return carried

    lax.fori_loop(0, planes_ref.shape[0], of_stop, 0)


def clear(ref):
    def step(i, carried):
        ref[i] = 0
        return carried

    lax.fori_loop(0, ref.shape[0], step, 0)


def make_listing(owner_ref, tile_ref, feather_ref, weight_ref, meta_ref, codes_ref, taken_ref):
    listed = feather_ref.shape[1]
    depth = meta_ref.shape[1]
    targets = meta_ref.shape[0] // (SLOT - EDGE)
    feather = feather_ref[...].astype(f32).astype(bf16)
    key = lax.broadcasted_iota(jnp.int32, (SROWS, depth), 0)
    lane = lax.broadcasted_iota(jnp.int32, (SROWS, depth), 1)
    codes_ref[...] = turned_dot(
        feather,
        (
            ((lane < OFFSETS) & (lane % SROWS == key))
            | ((lane == EDGE_WEIGHTS) & (key == SROWS - 1))
            | ((lane == EDGE_WEIGHTS + 1) & (key == 0))
        ).astype(bf16),
    )
    lines = listed * SROWS
    line = lax.broadcasted_iota(jnp.int32, (lines, listed), 0)
    chosen = (line // SROWS == lax.broadcasted_iota(jnp.int32, (lines, listed), 1)).astype(bf16)
    own = lax.broadcasted_iota(jnp.int32, (lines, SROWS), 1) == (
        lax.broadcasted_iota(jnp.int32, (lines, SROWS), 0) % SROWS
    )
    weight_ref[...] = dot(
        jnp.where(own, dot(chosen, feather, 1), 0.0).astype(bf16), jnp.ones((SROWS, depth), bf16)
    )
    meta_ref[...] = jnp.zeros(meta_ref.shape, f32)
    at = META - EDGE
    lane = lax.broadcasted_iota(jnp.int32, (1, depth), 1)

    def add(target, row):
        meta_ref[pl.ds(target * (SLOT - EDGE) + at, 1), :] += row

    def enter(entry, carried):
        owner, tile = owner_ref[entry], tile_ref[entry]
        rank = taken_ref[owner]
        taken_ref[owner] = rank + 1
        code = codes_ref[pl.ds(entry, 1), :]
        own = (lane < OFFSETS) & (lane // SROWS == rank)
        offset = jnp.where(lane == OFFSETS + rank, tile.astype(f32), 0.0)
        add(owner, jnp.where(own, code, offset))

        @pl.when((tile == TROWS - SROWS) & (owner + 1 < targets))
        def _():
            add(owner + 1, jnp.where(lane == EDGE_WEIGHTS, code, 0.0))

        @pl.when((tile == 0) & (owner > 0))
        def _():
            add(owner - 1, jnp.where(lane == EDGE_WEIGHTS + 1, code, 0.0))

        return carried

    clear(taken_ref)
    lax.fori_loop(0, listed, enter, 0)


def rows_of(stops, lines, depth, listed, targets):
    lengths = (stops * lines, lines, listed * SROWS, targets * (SLOT - EDGE), listed, stops * SROWS)
    at = [0]
    for length in lengths:
        at.append(at[-1] + length)
    return at


def prepare_kernel(
    count,
    owner_ref,
    source_ref,
    tile_ref,
    background_ref,
    relax_ref,
    estimate_ref,
    x_ref,
    y_ref,
    z_ref,
    feather_ref,
    measured_ref,
    planes_hbm,
    rows_hbm,
    planes_ref,
    log_ref,
    block_ref,
    weight_ref,
    meta_ref,
    places_ref,
    shares_ref,
    lines_x_ref,
    lines_y_ref,
    codes_ref,
    record_ref,
    taken_ref,
    sems,
    once_sems,
):
    stops, lines, depth = log_ref.shape
    rank = z_ref.shape[1] // depth
    copy = pltpu.make_async_copy(measured_ref.at[0], record_ref, once_sems.at[0])
    copy.start()

    place = lax.axis_index("view")

    def view_of(stop_id):
        return lax.rem(lax.rem(place + stop_id, count), z_ref.shape[0])

    def keep(stop_id):
        pairs = (
            (planes_ref.at[stop_id], planes_hbm.at[stop_id]),
            (
                log_ref.at[stop_id],
                rows_hbm.at[pl.ds(pl.multiple_of(stop_id * lines, SROWS), lines)],
            ),
        )
        return [
            pltpu.make_async_copy(source, target, sems.at[k, stop_id])
            for k, (source, target) in enumerate(pairs)
        ]

    key = lax.broadcasted_iota(jnp.int32, (1, depth), 1)

    def locate(entry, carried):
        row = jnp.where(key == 0, owner_ref[entry], tile_ref[entry])
        row = jnp.where(key == 1, source_ref[entry], row)
        places_ref[pl.ds(entry, 1), :] = row.astype(f32)
        return carried

    def share(stop_id, carried):
        own = lax.broadcasted_iota(jnp.int32, background_ref.shape, 1) == view_of(stop_id)
        for k, ref in enumerate((background_ref, relax_ref)):
            value = jnp.sum(jnp.where(own, ref[...].astype(f32), 0.0), axis=1, keepdims=True)
            shares_ref[pl.ds(stop_id * SROWS + k, 1), :] = jnp.broadcast_to(value, (1, depth))
        return carried

    lax.fori_loop(0, owner_ref.shape[0], locate, 0)
    lax.fori_loop(0, stops, share, 0)
    make_planes(view_of, x_ref, y_ref, z_ref, planes_ref, log_ref, lines_x_ref, lines_y_ref, keep)
    make_listing(owner_ref, tile_ref, feather_ref, weight_ref, meta_ref, codes_ref, taken_ref)
    copy.wait()
    block_ref[...] = visit(
        estimate_ref[...],
        record_ref[...],
        planes_ref.at[0],
        log_ref.at[0],
        shares_ref[:1],
        shares_ref[1:2],
    )
    at = rows_of(stops, lines, depth, owner_ref.shape[0], meta_ref.shape[0] // (SLOT - EDGE))
    finals = [
        pltpu.make_async_copy(ref, rows_hbm.at[pl.ds(first, ref.shape[0])], once_sems.at[k])
        for k, (ref, first) in enumerate(zip((block_ref, weight_ref, meta_ref, places_ref, shares_ref), at[1:]))
    ]
    for final in finals:
        final.start()

    def settle(stop_id, carried):
        for copy in keep(stop_id):
            copy.wait()
        return carried

    lax.fori_loop(0, stops, settle, 0)
    for final in finals:
        final.wait()


def prepare(count, listing, background, relax, estimate, kernel_x, kernel_y, kernel_z, feather, measured):
    views, rank, extent_x, _ = kernel_x.shape
    extent_y = kernel_y.shape[2]
    lines, depth = estimate.shape
    stops = measured.shape[0]
    wide = rank * lines
    listed = feather.shape[1]
    factors_x = kernel_x.transpose(1, 2, 0, 3).reshape(rank * extent_x * views, extent_x)
    planes = (stops, 2 * lines + 2 * depth, wide)
    rows = max(rows_of(stops, lines, depth, listed, count)[-1], 3 * stops * planes[1])
    return pl.pallas_call(
        functools.partial(prepare_kernel, count),
        out_shape=(jax.ShapeDtypeStruct(planes, bf16), jax.ShapeDtypeStruct((rows, depth), f32)),
        in_specs=[SMEM] * 3 + [VMEM] * 7 + [ANY],
        out_specs=[ANY] * 2,
        scratch_shapes=[
            pltpu.VMEM(planes, bf16),
            pltpu.VMEM((stops, lines, depth), f32),
            pltpu.VMEM((lines, depth), f32),
            pltpu.VMEM((listed * SROWS, depth), f32),
            pltpu.VMEM((count * (SLOT - EDGE), depth), f32),
            pltpu.VMEM((listed, depth), f32),
            pltpu.VMEM((stops * SROWS, depth), f32),
            pltpu.VMEM((extent_x * views, wide), f32),
            pltpu.VMEM((views * extent_y, wide), f32),
            pltpu.VMEM((listed, depth), f32),
            pltpu.VMEM((lines, depth), bf16),
            pltpu.SMEM((count,), jnp.int32),
            pltpu.SemaphoreType.DMA((2, stops)),
            pltpu.SemaphoreType.DMA((5,)),
        ],
        compiler_params=WHOLE,
        cost_estimate=pl.CostEstimate(
            flops=views * 8 * lines * wide, bytes_accessed=views * 8 * lines * wide, transcendentals=0
        ),
    )(*listing, background, relax, estimate, factors_x, kernel_y, kernel_z, feather, measured)


def stage_kernel(start, planes_hbm, rows_hbm, planes_ref, rows_ref, log_ref, sems):
    copies = [
        pltpu.make_async_copy(source, target, sems.at[k])
        for k, (source, target) in enumerate(
            (
                (planes_hbm.at[1], planes_ref),
                (rows_hbm.at[pl.ds(start, rows_ref.shape[0])], rows_ref),
                (rows_hbm.at[pl.ds(log_ref.shape[0], log_ref.shape[0])], log_ref),
            )
        )
    ]
    for copy in copies:
        copy.start()
    for copy in copies:
        copy.wait()


def stage(planes, rows, at):
    depth = rows.shape[1]
    return pl.pallas_call(
        functools.partial(stage_kernel, at[1]),
        out_shape=(
            jax.ShapeDtypeStruct(planes.shape[1:], bf16),
            jax.ShapeDtypeStruct((at[-1] - at[1], depth), f32),
            jax.ShapeDtypeStruct((at[2] - at[1], depth), f32),
        ),
        in_specs=[ANY] * 2,
        out_specs=[VMEM] * 3,
        scratch_shapes=[pltpu.SemaphoreType.DMA((3,))],
        compiler_params=NEAR,
    )(planes, rows)


def stops_kernel(
    by_host,
    count,
    listed,
    records_ref,
    first_planes_ref,
    near_ref,
    first_log_ref,
    planes_hbm,
    rows_hbm,
    block_ref,
    send_ref,
    planes_ref,
    log_ref,
    places_ref,
    taken_ref,
    sems,
    once_sems,
):
    stops, lines, depth = log_ref.shape
    targets = send_ref.shape[0]
    at = rows_of(stops, lines, depth, listed, targets)
    position = lax.axis_index("view")

    groups = [(2, 1)]
    while sum(groups[-1]) < stops:
        first = sum(groups[-1])
        groups.append((first, min(len(groups) + 1, stops - first)))

    def near(part):
        return near_ref[at[part] - at[1] : at[part + 1] - at[1], :]

    def log_in(stop_id):
        return pltpu.make_async_copy(
            rows_hbm.at[pl.ds(stop_id * lines, lines)], log_ref.at[stop_id], sems.at[1, stop_id]
        )

    def arrivals(group):
        first, length = groups[group]
        copies = [
            pltpu.make_async_copy(
                planes_hbm.at[pl.ds(first, length)],
                planes_ref.at[pl.ds(first, length)],
                sems.at[0, group],
            )
        ]
        return copies + [log_in(stop_id) for stop_id in range(first, first + length)]

    places_in = pltpu.make_async_copy(
        rows_hbm.at[pl.ds(at[4], listed)], places_ref, once_sems.at[0]
    )
    for group in range(len(groups)):
        for copy in arrivals(group):
            copy.start()
    places_in.start()
    clear(taken_ref)
    send_ref[:, :EDGE, :] = jnp.zeros((targets, EDGE, depth), f32)
    send_ref[:, EDGE:, :] = near(3).reshape(targets, SLOT - EDGE, depth)

    def advance(stop_id, block):
        host = lax.rem(position + stop_id, count)
        share = at[5] - at[1] + stop_id * SROWS
        return visit(
            block,
            records_ref[host if by_host else stop_id],
            first_planes_ref if stop_id == 1 else planes_ref.at[stop_id],
            first_log_ref if stop_id == 1 else log_ref.at[stop_id],
            near_ref[share : share + 1, :],
            near_ref[share + 1 : share + 2, :],
        )

    block = advance(1, near(1))
    for group, (first, length) in enumerate(groups):
        for copy in arrivals(group):
            copy.wait()
        for stop_id in range(first, first + length):
            block = advance(stop_id, block)
    block_ref[...] = block
    places_in.wait()

    def place(entry, carried):
        owner, source, tile = (places_ref[entry, k].astype(jnp.int32) for k in range(3))
        rank = taken_ref[owner]
        taken_ref[owner] = rank + 1
        weights = near_ref[pl.ds(pl.multiple_of(at[2] - at[1] + entry * SROWS, SROWS), SROWS), :]
        piece = block_ref[pl.ds(source, SROWS), :] * weights
        send_ref[owner, pl.ds(pl.multiple_of(rank * SROWS, SROWS), SROWS), :] = piece

        @pl.when((tile == TROWS - SROWS) & (owner + 1 < targets))
        def _():
            send_ref[owner + 1, EDGE : EDGE + 1, :] += piece[SROWS - 1 :]

        @pl.when((tile == 0) & (owner > 0))
        def _():
            send_ref[owner - 1, EDGE + 1 : EDGE + 2, :] += piece[:1]

        return carried

    lax.fori_loop(0, listed, place, 0)


def run_stops(by_host, count, listed, records, planes, rows):
    stops, lines, depth = records.shape
    first_planes, near, first_log = stage(planes, rows, rows_of(stops, lines, depth, listed, count))
    return pl.pallas_call(
        functools.partial(stops_kernel, by_host, count, listed),
        out_shape=(
            jax.ShapeDtypeStruct((lines, depth), f32),
            jax.ShapeDtypeStruct((count, SLOT, depth), f32),
        ),
        in_specs=[VMEM] * 4 + [ANY] * 2,
        out_specs=(VMEM, VMEM),
        scratch_shapes=[
            pltpu.VMEM(planes.shape, planes.dtype),
            pltpu.VMEM((stops, lines, depth), f32),
            pltpu.SMEM((listed, depth), f32),
            pltpu.SMEM((count,), jnp.int32),
            pltpu.SemaphoreType.DMA((2, stops)),
            pltpu.SemaphoreType.DMA((1,)),
        ],
        compiler_params=NEAR,
    )(records, first_planes, near, first_log, planes, rows)


def blend_kernel(data_ref, block_ref, smoothed_ref, refined_hbm, sem):
    refined_out = pltpu.make_async_copy(block_ref, refined_hbm, sem)
    refined_out.start()
    count, _, depth = data_ref.shape
    place = lax.axis_index("view")
    slots = count * EDGE
    meta = data_ref[:, META, :]
    key = lax.broadcasted_iota(jnp.int32, (depth, slots), 0)
    column = lax.broadcasted_iota(jnp.int32, (depth, slots), 1) % EDGE
    spread_weight = (key == column).astype(bf16)
    spread_offset = (key == OFFSETS + column // SROWS).astype(bf16)
    own = lax.broadcasted_iota(jnp.int32, (count, slots), 0) == (
        lax.broadcasted_iota(jnp.int32, (count, slots), 1) // EDGE
    )
    coded = meta.astype(bf16)
    weight = jnp.sum(jnp.where(own, dot(coded, spread_weight), 0.0), axis=0, keepdims=True)
    offset = jnp.sum(jnp.where(own, dot(coded, spread_offset), 0.0), axis=0, keepdims=True)
    line = offset.astype(jnp.int32) + lax.broadcasted_iota(jnp.int32, (1, slots), 1) % SROWS
    placed = (line == lax.broadcasted_iota(jnp.int32, (TROWS, slots), 0)).astype(f32)
    data = data_ref[:, :EDGE, :].reshape(slots, depth)
    numerator = 1.0 + jnp.dot(
        placed, data, preferred_element_type=f32, precision=lax.Precision.HIGHEST
    )
    denominator = 1.0 + jnp.sum(placed * weight, axis=1, keepdims=True)
    joined = numerator / denominator

    def edge(which, inside):
        top = 1.0 + jnp.sum(data_ref[:, EDGE + which, :], axis=0, keepdims=True)
        lane = EDGE_WEIGHTS + which
        below = 1.0 + jnp.sum(meta[:, lane : lane + 1], axis=0, keepdims=True)
        return jnp.where(inside, top / below, 0.0)

    behind = edge(0, place > 0)
    beyond = edge(1, place < count - 1)
    side = jnp.zeros((TROWS, 1), f32)
    flux = jnp.zeros_like(joined)
    for neighbor in (
        jnp.concatenate([joined[1:], beyond], axis=0),
        jnp.concatenate([behind, joined[:-1]], axis=0),
        jnp.concatenate([joined[:, 1:], side], axis=1),
        jnp.concatenate([side, joined[:, :-1]], axis=1),
    ):
        change = neighbor - joined
        flux = flux + change / (1.0 + change / edge_scale * (change / edge_scale))
    smoothed_ref[...] = joined + smooth_rate * flux
    refined_out.wait()


def blend(data, block):
    return pl.pallas_call(
        blend_kernel,
        out_shape=(
            jax.ShapeDtypeStruct((TROWS, data.shape[2]), f32),
            jax.ShapeDtypeStruct(block.shape, f32),
        ),
        in_specs=[VMEM] * 2,
        out_specs=(VMEM, ANY),
        scratch_shapes=[pltpu.SemaphoreType.DMA],
        compiler_params=pltpu.CompilerParams(vmem_limit_bytes=32 << 20),
    )(data, block)


def on_device(
    estimate,
    measured,
    kernel_z,
    kernel_x,
    kernel_y,
    background,
    relax,
    owner,
    source_offset,
    tile_offset,
    feather,
):
    count = lax.axis_size("view")
    stops = measured.shape[0]
    views, rank, depth, _ = kernel_z.shape
    by_host = stops == count
    if by_host:
        records = lax.all_to_all(
            by_target(measured), "view", split_axis=0, concat_axis=0, tiled=True
        )
    else:
        arrived = [measured[0]]
        for stop_id in range(1, stops):
            route = [((i + stop_id) % count, i) for i in range(count)]
            arrived.append(lax.ppermute(measured[stop_id], "view", route))
        records = jnp.stack(arrived, axis=0)

    factors_z = kernel_z.reshape(views, rank * depth, depth)
    planes, rows = prepare(
        count,
        (owner[:, 0], source_offset, tile_offset),
        background[None],
        relax[None],
        estimate,
        kernel_x,
        kernel_y,
        factors_z,
        feather.T,
        measured,
    )
    block, outgoing = run_stops(by_host, count, feather.shape[0], records, planes, rows)
    incoming = lax.all_to_all(outgoing, "view", split_axis=0, concat_axis=0, tiled=True)
    smoothed, refined = blend(incoming, block)
    return refined, smoothed


def solution(mesh):
    lined = P(("groups", "view"))
    return jax.shard_map(
        on_device,
        mesh=mesh,
        in_specs=(
            P(("groups", "view"), None),
            P(("groups", "view"), None, None),
            P(),
            P(),
            P(),
            P(),
            P(),
            P(("groups", "view"), None),
            lined,
            lined,
            P(("groups", "view"), None),
        ),
        out_specs=(P(("groups", "view"), None), P(("groups", "view"), None)),
        check_vma=False,
    )
```
